128 devices in a mesh: patch: 32 (over x, z, y_hi), head: 4 (over y_lo, core).
Axes of the slice: x: 4, y: 4 (y_hi: 2, y_lo: 2; y = y_hi * 2 + y_lo), z: 4, core: 2. Of those that a mesh axis runs over, the one named last changes fastest.
Arguments:
- hidden: bfloat16 [4, 12, 512, 2560], P(None, None, 'patch', 'head'), may hold values from -6 to 6
- qkv_first: bfloat16 [3, 4, 12, 512, 2560], P(None, None, None, 'patch', 'head'), may hold values from -60 to 60
- wo_first: bfloat16 [2560, 2560], P('patch', 'head'), may hold values from -0.5 to 0.5
- norm_gain: float32 [2560], replicated, may hold values from 0.5 to 4
- wqkv_second: bfloat16 [2560, 3, 2560], P('patch', None, 'head'), may hold values from -3 to 3
- wo_second: bfloat16 [2560, 2560], P('patch', 'head'), may hold values from -0.5 to 0.5
- tile_clip: int32 [32], replicated, may hold values from 0 to 7, never falling along the last dimension, each value on 1 to 8 neighbouring positions
- clip_frames: int32 [8], replicated, may hold values from 1 to 4, as said below
Outputs:
- refined: float32 [4, 12, 512, 2560], P(None, None, 'patch', 'head')
The draws below stay inside these ranges and needn't reach their ends.
Inputs may be any that keep to these rules, and one draw needn't show every extreme that they name: tile_clip never falls along the tiles; each clip covers a run of neighbouring tiles, at most 8 of them. `clip_frames`: one clip has all 4 frames.
All inputs are finite; a program needn't handle non-finite values.
Results may differ from the reference program's by a relative error of at most 0.015.
Values may be sent and summed in bfloat16 or wider, within the bound.
No kernel may reach another device: no remote copies, remote signals or barrier semaphores. Data moves between devices by JAX's collectives and lax.ppermute only.
A program may use at most 128 MiB of HBM per device.

```python
import math
import jax
import jax.numpy as jnp
import numpy as np
from jax import lax

D = 2560
HEADS = 20
HD = 128
TILE_F = 4
TILE_H = 12
WIN_F = 2
WIN_W = 16
NW = 512
CLIPS = 8
N_PATCH = 32
N_HEAD = 4


def draw_qkv_first(key, part):
    key = jax.random.fold_in(key, 11)
    key_one = jax.random.fold_in(key, 0)
    shape = (3, TILE_F, TILE_H, NW, D)
    values_all = jnp.clip(jax.random.normal(key_one, shape, jnp.float32), -6.0, 6.0)
    return values_all.astype(jnp.bfloat16)


def draw_norm_gain(key, part):
    key = jax.random.fold_in(key, 23)
    gains = jax.random.uniform(key, (D,), jnp.float32, 0.5, 1.5)
    return gains


def draw_clip_frames(key, part):
    key = jax.random.fold_in(key, 29)
    key_one, key_two = jax.random.split(key)
    counts = jax.random.randint(key_one, (CLIPS,), 1, TILE_F // 2 + 1)
    largest = jax.random.randint(key_two, (), 0, CLIPS)
    return jnp.where(jnp.arange(CLIPS) == largest, TILE_F, counts).astype(jnp.int32)


def draw_wqkv_second(key, part):
    key = jax.random.fold_in(key, 37)
    key_one = jax.random.fold_in(key, 0)
    spread = D ** (-0.5)
    weights = jnp.clip(jax.random.normal(key_one, (D, 3, D), jnp.float32), -6.0, 6.0) * spread
    return weights.astype(jnp.bfloat16)


def block_scale(own_key, dims, cuts, low, top_value):
    factor_of = 1.0
    for dim, parts in cuts:
        steps = jax.random.uniform(jax.random.fold_in(jax.random.fold_in(own_key, 6), dim), (parts,), jnp.float32, low / len(cuts), top_value / len(cuts))
        factor_of = factor_of * jnp.repeat(jnp.exp(steps), dims[dim] // parts).reshape((-1,) + (1,) * (len(dims) - 1 - dim))
    return factor_of


def split_up(count, total, bound, lean):
    weights = [(1 << 20) // math.isqrt(rank ** lean) + 1 for rank in range(2, count + 1)]
    spare, holding = total - bound - (count - 1), [1] * (count - 1)
    while spare > 0:
        movable = [i for i in range(count - 1) if holding[i] < bound]
        mass, left = sum([weights[i] for i in movable]), spare
        for i in movable:
            more = min(bound - holding[i], max(1, left * weights[i] // mass), spare)
            holding[i] = holding[i] + more
            spare = spare - more
    return np.array([bound] + holding)


def ragged(own_key, number_of, total, bound, skew):
    if number_of == 2:
        one = jax.random.randint(own_key, (), max(1, total - bound), min(bound, total - 1) + 1)
        return jnp.stack([one, total - one])
    lengths = jnp.asarray(split_up(number_of, total, bound, skew), jnp.int32)
    pairs = (number_of - 1) // 2
    source_of, taker = lengths[1:1 + 2 * pairs:2], lengths[2:2 + 2 * pairs:2]
    margin = jnp.minimum(source_of - 1, bound - taker)
    moved = jax.random.randint(jax.random.fold_in(own_key, 1), (pairs,), 0, 1 << 20) % (margin + 1)
    lengths = lengths.at[1:1 + 2 * pairs:2].set(source_of - moved).at[2:2 + 2 * pairs:2].set(taker + moved)
    return lengths[jax.random.permutation(jax.random.fold_in(own_key, 2), number_of)]


def normal_values(key, dims, scale, bound, cuts=(), kind=jnp.bfloat16):
    factor_of = block_scale(key, dims, cuts, -0.22, 0.18) if cuts else 1.0
    result = jax.random.normal(key, dims, jnp.float32) * scale * factor_of
    return jnp.minimum(jnp.maximum(result, -bound), bound).astype(kind)


def setup_inputs(seed: int = 0) -> dict:
    arg_keys = jax.random.split(jax.random.key(seed), 9)
    hidden = normal_values(arg_keys[0], (TILE_F, TILE_H, NW, D), 1.0, 6.0, ((2, 32), (3, 4)))
    qkv_first = draw_qkv_first(jax.random.fold_in(arg_keys[8], 71), 0)
    wo_first = normal_values(arg_keys[2], (D, D), HD ** -0.5, 0.5, ((0, 32), (1, 4)))
    norm_gain = draw_norm_gain(jax.random.fold_in(arg_keys[8], 71), 0)
    wqkv_second = draw_wqkv_second(jax.random.fold_in(arg_keys[8], 71), 0)
    wo_second = normal_values(arg_keys[5], (D, D), HD ** -0.5, 0.5, ((0, 32), (1, 4)))
    tile_clip = jnp.searchsorted(jnp.cumsum(ragged(arg_keys[6], CLIPS, N_PATCH, min(8, N_PATCH - CLIPS + 1), 1)), jnp.arange(N_PATCH), side="right").astype(jnp.int32)
    clip_frames = draw_clip_frames(jax.random.fold_in(arg_keys[8], 71), 0)
    return {"hidden": hidden, "qkv_first": qkv_first, "wo_first": wo_first, "norm_gain": norm_gain, "wqkv_second": wqkv_second, "wo_second": wo_second, "tile_clip": tile_clip, "clip_frames": clip_frames}


EPSILON = 1e-06
MASKED_SCORE = -1e+30

def window_split(x, frames_win, cols_win):
    frames, height, across = (x.shape[0], x.shape[1], x.shape[2])
    trailing = x.shape[3:]
    grouped = x.reshape((frames // frames_win, frames_win, height, across // cols_win, cols_win) + trailing)
    order_dims = (0, 3, 1, 2, 4) + tuple(range(5, 5 + len(trailing)))
    grouped = jnp.transpose(grouped, order_dims)
    return grouped.reshape((frames // frames_win * (across // cols_win), frames_win * height * cols_win) + trailing)

def window_merge(grouped, frames, height, across, frames_win, cols_win):
    trailing = grouped.shape[2:]
    grouped = grouped.reshape((frames // frames_win, across // cols_win, frames_win, height, cols_win) + trailing)
    order_dims = (0, 2, 3, 1, 4) + tuple(range(5, 5 + len(trailing)))
    grouped = jnp.transpose(grouped, order_dims)
    return grouped.reshape((frames, height, across) + trailing)

def window_attention(query_part, key_part, value_part, live_mask, clip_cols):
    frames, height, across = query_part.shape[:3]
    head_dim = query_part.shape[-1]
    live_tok = jnp.broadcast_to(live_mask[:, None, :], (frames, height, across))
    clip_tok = jnp.broadcast_to(clip_cols[None, None, :], (frames, height, across))
    query_win = window_split(query_part, WIN_F, WIN_W).astype(jnp.float32)
    key_win = window_split(key_part, WIN_F, WIN_W).astype(jnp.float32)
    value_win = window_split(value_part, WIN_F, WIN_W).astype(jnp.float32)
    live_win = window_split(live_tok, WIN_F, WIN_W)
    clip_win = window_split(clip_tok, WIN_F, WIN_W)
    scores = jnp.einsum('nqhd,nkhd->nhqk', query_win, key_win) * (1.0 / math.sqrt(head_dim))
    allowed = (clip_win[:, :, None] == clip_win[:, None, :]) & live_win[:, None, :]
    scores = jnp.where(allowed[:, None], scores, MASKED_SCORE)
    row_max = lax.optimization_barrier(jnp.max(scores, axis=-1, keepdims=True))
    lifted = jnp.exp(scores - row_max)
    weights = (lifted / lax.optimization_barrier(jnp.sum(lifted, axis=-1, keepdims=True))).astype(jnp.bfloat16)
    context = jnp.einsum('nhqk,nkhd->nqhd', weights.astype(jnp.float32), value_win)
    context = jnp.where(live_win[:, :, None, None], context, 0.0).astype(jnp.bfloat16)
    return window_merge(context, frames, height, across, WIN_F, WIN_W)

def project(context, weight):
    model_width = context.shape[1]
    group_cols = model_width // N_HEAD
    summed = jnp.zeros((context.shape[0], model_width), jnp.float32)
    for group in range(N_HEAD):
        lower = group * group_cols
        piece = jnp.dot(context[:, lower:lower + group_cols], weight[:, lower:lower + group_cols].T, preferred_element_type=jnp.float32)
        summed = summed + piece
    return summed

def reference(hidden, qkv_first, wo_first, norm_gain, wqkv_second, wo_second, tile_clip, clip_frames):
    frames, height, across, model_width = hidden.shape
    head_count = HEADS
    head_dim = HD
    tile_width = across // N_PATCH
    col_tile = (jnp.arange(across, dtype=jnp.int32) // tile_width).astype(jnp.int32)
    clip_col = tile_clip[col_tile]
    frames_col = clip_frames[clip_col]
    live_mask = jnp.arange(frames, dtype=jnp.int32)[:, None] < frames_col[None, :]

    def split_heads(x):
        return jnp.moveaxis(x.reshape(frames, height, across, head_count, head_dim), 3, 0)

    def first_head(inputs):
        query_part, key_part, value_part = inputs
        return window_attention(query_part[..., None, :], key_part[..., None, :], value_part[..., None, :], live_mask, clip_col)[..., 0, :]
    context_first = lax.map(first_head, (split_heads(qkv_first[0]), split_heads(qkv_first[1]), split_heads(qkv_first[2])))
    context_first = jnp.moveaxis(context_first, 0, 3).reshape(-1, model_width)
    hidden_rows = hidden.reshape(-1, model_width)
    block_first = hidden_rows.astype(jnp.float32) + project(context_first, wo_first)
    normed = (block_first * lax.rsqrt(lax.optimization_barrier(jnp.mean(block_first * block_first, axis=-1, keepdims=True)) + EPSILON) * norm_gain).astype(jnp.bfloat16)
    shift_f = WIN_F // 2
    shift_w = WIN_W // 2
    live_rolled = jnp.roll(jnp.roll(live_mask, -shift_f, axis=0), -shift_w, axis=1)
    clip_rolled = jnp.roll(clip_col, -shift_w)
    weight_heads = jnp.transpose(wqkv_second.reshape(model_width, 3, head_count, head_dim), (2, 0, 1, 3))

    def second_head(weight_head):
        projected = jnp.dot(normed, weight_head.reshape(model_width, 3 * head_dim), preferred_element_type=jnp.float32)
        projected = projected.astype(jnp.bfloat16).reshape(frames, height, across, 3, head_dim)
        projected = jnp.roll(jnp.roll(projected, -shift_f, axis=0), -shift_w, axis=2)
        shifted = window_attention(projected[..., 0, :][..., None, :], projected[..., 1, :][..., None, :], projected[..., 2, :][..., None, :], live_rolled, clip_rolled)
        shifted = jnp.roll(jnp.roll(shifted, shift_f, axis=0), shift_w, axis=2)
        return shifted[..., 0, :]
    context_second = lax.map(second_head, weight_heads)
    context_second = jnp.moveaxis(context_second, 0, 3).reshape(-1, model_width)
    refined = block_first + project(context_second, wo_second)
    return refined.reshape(frames, height, across, model_width)
```

```python
import math

import jax
import jax.numpy as jnp
from jax import lax
from jax.experimental import pallas as pl
from jax.experimental.pallas import tpu as pltpu
from jax.sharding import PartitionSpec as P

HD = 128
EPSILON = 1e-06
MASKED_SCORE = -1e30
EXP2_SCALE = math.log2(math.e) / math.sqrt(HD)
BF16 = jnp.bfloat16
F32 = jnp.float32
AXES = ("patch", "head")
NX, NZ, NPATCH, NDEV = 4, 4, 32, 128
VMEM_LIMIT = 40 * 1024 * 1024

I_C, I_YL, I_X, I_Z, I_OWN, I_NEXT, I_SAME = range(7)


def device_of(x, z, yh, yl, c):
    return ((((x % NX) * NZ + z % NZ) * 2 + yh % 2) * 2 + yl % 2) * 2 + c % 2


def route(dx=0, dz=0, dyh=0, dyl=0, dc=0):
    pairs = []
    for i in range(NDEV):
        c, yl, yh, z, x = i % 2, i // 2 % 2, i // 4 % 2, i // 8 % 4, i // 32
        pairs.append((i, device_of(x + dx, z + dz, yh + dyh, yl + dyl, c + dc)))
    return pairs


def tile_route(step, flip):
    return [(i, ((i + 4 * step) % NDEV) ^ (2 * flip)) for i in range(NDEV)]


def send(block, pairs):
    return lax.ppermute(block, AXES, pairs)


def params(**more):
    return pltpu.CompilerParams(vmem_limit_bytes=VMEM_LIMIT, **more)


def softmax_values(scores, values):
    top = jnp.max(scores, axis=-1, keepdims=True)
    lifted = jnp.exp2((scores - top) * EXP2_SCALE)
    total = jnp.sum(lifted, axis=-1, keepdims=True)
    context = jnp.dot(lifted.astype(BF16), values, preferred_element_type=F32)
    return context / total


def scores_of(query, key):
    return lax.dot_general(query, key, (((1,), (1,)), ((), ())), preferred_element_type=F32)


def aligned_kernel(info, qkv, out_near, out_far):
    frames_own = info[I_OWN]
    lane = lax.broadcasted_iota(jnp.int32, (1, 384), 1) // 192
    row = lax.broadcasted_iota(jnp.int32, (384, 1), 0) // 192
    for window in range(2):
        rows = slice(window * 384, window * 384 + 384)
        scores = scores_of(qkv[0, rows], qkv[1, rows])
        scores = jnp.where(2 * window + lane < frames_own, scores, MASKED_SCORE)
        context = softmax_values(scores, qkv[2, rows])
        context = jnp.where(2 * window + row < frames_own, context, 0.0)
        context = context.reshape(2, 12, 16, HD)
        for half in range(2):
            place = (2 * window + half + 3) % 4
            out_near[place] = context[half, :, :8].reshape(96, HD).astype(BF16)
            out_far[place] = context[half, :, 8:].reshape(96, HD).astype(BF16)


def aligned_attention(info, qkv):
    heads = qkv.shape[-1] // HD
    spec = pl.BlockSpec((4, 96, HD), lambda j, s: (0, 0, j))
    shape = jax.ShapeDtypeStruct((4, 96, heads * HD), BF16)
    return pl.pallas_call(
        aligned_kernel,
        grid_spec=pltpu.PrefetchScalarGridSpec(
            num_scalar_prefetch=1,
            grid=(heads,),
            in_specs=[pl.BlockSpec((3, 768, HD), lambda j, s: (0, 0, j))],
            out_specs=[spec, spec],
        ),
        out_shape=[shape, shape],
        compiler_params=params(),
        cost_estimate=pl.CostEstimate(flops=1510000000, bytes_accessed=4000000, transcendentals=1500000),
        name="aligned_attention",
    )(info, qkv)


def order_of(i, info):
    c = info[I_C]
    return 2 * (i % 2) + jnp.where(i < 2, 1 - c, c)


def project_rows(i, info, rows, weight, extra, out_send, out_keep):
    part = lax.dot_general(
        rows, weight[...], (((1,), (1,)), ((), ())), preferred_element_type=F32
    )

    @pl.when(i < 2)
    def _():
        out_send[...] = part.astype(BF16)

    @pl.when(i >= 2)
    def _():
        mine = jnp.where(i - 2 == info[I_YL], 1.0, 0.0)
        out_keep[...] = part + mine * extra


def project_first_kernel(info, far, near, weight, hid_far, hid_near, out_send, out_keep):
    rows = jnp.concatenate([far[...].reshape(192, 640), near[...].reshape(192, 640)], axis=0)
    extra = jnp.concatenate(
        [hid_far[...].reshape(192, 640), hid_near[...].reshape(192, 640)], axis=0
    ).astype(F32)
    project_rows(pl.program_id(0), info, rows, weight, extra, out_send, out_keep)


def project_second_kernel(info, rows, weight, block, out_send, out_keep):
    project_rows(pl.program_id(0), info, rows[...], weight, block[...], out_send, out_keep)


def project_call(kernel, info, operands, specs, name):
    return pl.pallas_call(
        kernel,
        grid_spec=pltpu.PrefetchScalarGridSpec(
            num_scalar_prefetch=1,
            grid=(4,),
            in_specs=specs,
            out_specs=[
                pl.BlockSpec((384, 640), lambda i, s: (0, jnp.minimum(i, 1))),
                pl.BlockSpec((384, 640), lambda i, s: (0, jnp.maximum(i - 2, 0))),
            ],
        ),
        out_shape=[
            jax.ShapeDtypeStruct((384, 1280), BF16),
            jax.ShapeDtypeStruct((384, 1280), F32),
        ],
        compiler_params=params(),
        cost_estimate=pl.CostEstimate(flops=1260000000, bytes_accessed=7000000, transcendentals=0),
        name=name,
    )(info, *operands)


def project_first(info, window, far, near, weight, hid_far, hid_near):
    half = pl.BlockSpec((2, 96, 640), lambda i, s: (window, 0, 0))
    weight_spec = pl.BlockSpec((640, 640), lambda i, s: (order_of(i, s), 0))
    return project_call(
        project_first_kernel,
        info,
        (far, near, weight, hid_far, hid_near),
        [half, half, weight_spec, half, half],
        "project_first",
    )


def project_second(info, rows, weights, full):
    specs = [
        pl.BlockSpec((384, 640), lambda i, s: (0, 0)),
        pl.BlockSpec((640, 640), lambda i, s: (order_of(i, s), 3)),
        pl.BlockSpec((384, 640), lambda i, s: (0, s[I_YL])),
    ]
    return project_call(
        project_second_kernel, info, (rows, weights, full), specs, "project_second"
    )


def shifted_kernel(window, info, own, other, gain, weight, out, normed, qkv):
    j = pl.program_id(0)
    c = info[I_C]

    @pl.when(j == 0)
    def _():
        mine = own[...]
        theirs = other[...].astype(F32)
        squares = jnp.sum(mine * mine, axis=-1, keepdims=True) + jnp.sum(
            theirs * theirs, axis=-1, keepdims=True
        )
        scale = lax.rsqrt(squares * (1.0 / 2560) + EPSILON)
        for a in range(2):
            for source, core in ((mine, c), (theirs, 1 - c)):
                lower = pl.multiple_of((2 * a + core) * 640, 128)
                part = source[:, a * 640 : (a + 1) * 640] * scale * gain[:, pl.ds(lower, 640)]
                normed[:, pl.ds(lower, 640)] = part.astype(BF16)

    qkv[j] = jnp.dot(normed[...], weight[...], preferred_element_type=F32).astype(BF16)

    @pl.when(j == 2)
    def _():
        first, second = ((1, 2), (3, 0))[window]
        lane = lax.broadcasted_iota(jnp.int32, (1, 384), 1)
        row = lax.broadcasted_iota(jnp.int32, (384, 1), 0)

        def live(position):
            frame = jnp.where(position // 96 % 2 == 0, first, second)
            frames = jnp.where(position < 192, info[I_OWN], info[I_NEXT])
            return frame < frames

        alike = ((lane < 192) == (row < 192)) | (info[I_SAME] > 0)
        allowed = alike & live(lane)
        live_rows = live(row)
        for head in range(5):
            cols = slice(head * HD, head * HD + HD)
            scores = scores_of(qkv[0, :, cols], qkv[1, :, cols])
            scores = jnp.where(allowed, scores, MASKED_SCORE)
            context = softmax_values(scores, qkv[2, :, cols])
            out[:, cols] = jnp.where(live_rows, context, 0.0).astype(BF16)


def shifted_attention(info, window, own, other, gain, weights):
    def whole(shape):
        return pl.BlockSpec(shape, lambda j, s: (0, 0))

    return pl.pallas_call(
        lambda *refs: shifted_kernel(window, *refs),
        grid_spec=pltpu.PrefetchScalarGridSpec(
            num_scalar_prefetch=1,
            grid=(3,),
            in_specs=[
                whole((384, 1280)),
                whole((384, 1280)),
                whole((1, 2560)),
                pl.BlockSpec((2560, 640), lambda j, s: (0, j)),
            ],
            out_specs=whole((384, 640)),
            scratch_shapes=[pltpu.VMEM((384, 2560), BF16), pltpu.VMEM((3, 384, 640), BF16)],
        ),
        out_shape=jax.ShapeDtypeStruct((384, 640), BF16),
        compiler_params=params(),
        cost_estimate=pl.CostEstimate(
            flops=4200000000, bytes_accessed=14000000, transcendentals=800000
        ),
        name="shifted_attention",
    )(info, own, other, gain, weights)


def split_kernel(info, keep_mine, recv_mine, keep_pair, recv_pair, own, to_pair, next_same, next_cross):
    mine = keep_mine[...] + recv_mine[...].astype(F32)
    pair = keep_pair[...] + recv_pair[...].astype(F32)
    own[...] = mine[:192]
    to_pair[...] = pair[:192].astype(BF16)
    next_same[...] = mine[192:].astype(BF16)
    next_cross[...] = pair[192:].astype(BF16)


def split_rows(info, keep, recv):
    mine = pl.BlockSpec((384, 640), lambda i, s: (0, s[I_YL]))
    pair = pl.BlockSpec((384, 640), lambda i, s: (0, 1 - s[I_YL]))
    whole = pl.BlockSpec((192, 640), lambda i, s: (0, 0))
    low = jax.ShapeDtypeStruct((192, 640), BF16)
    return pl.pallas_call(
        split_kernel,
        grid_spec=pltpu.PrefetchScalarGridSpec(
            num_scalar_prefetch=1,
            grid=(1,),
            in_specs=[mine, mine, pair, pair],
            out_specs=[whole] * 4,
        ),
        out_shape=[jax.ShapeDtypeStruct((192, 640), F32), low, low, low],
        compiler_params=params(),
        cost_estimate=pl.CostEstimate(flops=500000, bytes_accessed=4000000, transcendentals=0),
        name="split_rows",
    )(info, keep, recv, keep, recv)


def final_kernel(*refs):
    out = refs[-1]
    for window in range(2):
        own, pair, same, cross = [ref[...] for ref in refs[4 * window : 4 * window + 4]]
        far = (own + pair.astype(F32)).reshape(2, 12, 8, HD)
        near = (same.astype(F32) + cross.astype(F32)).reshape(2, 12, 8, HD)
        for half in range(2):
            out[(2 * window + half + 1) % 4] = jnp.concatenate([near[half], far[half]], axis=1)


def final_rows(operands):
    spec = pl.BlockSpec((192, HD), lambda j: (0, j))
    return pl.pallas_call(
        final_kernel,
        grid=(5,),
        in_specs=[spec] * 8,
        out_specs=pl.BlockSpec((4, 12, 16, HD), lambda j: (0, 0, 0, j)),
        out_shape=jax.ShapeDtypeStruct((4, 12, 16, 640), F32),
        compiler_params=params(),
        cost_estimate=pl.CostEstimate(flops=1000000, bytes_accessed=5000000, transcendentals=0),
        name="final_rows",
    )(*operands)


def place_kernel(info, *refs):
    pieces, out, sems = refs[:8], refs[8], refs[9]
    x, z = info[I_X], info[I_Z]
    copies = []
    for lane in range(2):
        for outer in range(4):
            for inner in range(4):
                k, j = (outer, inner) if lane == 0 else (inner, outer)
                start = ((x + k) % 4) * 640 + ((z + j) % 4) * 160 + 80 * lane
                copies.append(
                    pltpu.make_async_copy(
                        pieces[4 * lane + outer].at[pl.ds(inner * 80, 80)],
                        out.at[pl.ds(pl.multiple_of(start, 16), 80)],
                        sems.at[len(copies)],
                    )
                )
    for copy in copies:
        copy.start()
    for copy in copies:
        copy.wait()


def place_rows(info, pieces, cols):
    anywhere = pl.BlockSpec(memory_space=pl.ANY)
    return pl.pallas_call(
        place_kernel,
        grid_spec=pltpu.PrefetchScalarGridSpec(
            num_scalar_prefetch=1,
            grid=(1,),
            in_specs=[anywhere] * 8,
            out_specs=anywhere,
            scratch_shapes=[pltpu.SemaphoreType.DMA((32,))],
        ),
        out_shape=jax.ShapeDtypeStruct((2560, cols), BF16),
        compiler_params=params(),
        cost_estimate=pl.CostEstimate(flops=0, bytes_accessed=6600000, transcendentals=0),
        name="place_rows",
    )(info, *pieces)


def ring(block, axis):
    ahead = send(block, route(**{axis: -1}))
    behind = send(block, route(**{axis: 1}))
    across = send(block, route(**{axis: 2}))
    return [block, ahead, across, behind]


def gather_rows(info, low, high):
    along_z = jnp.concatenate(ring(low, "dz"), axis=0)
    along_x = jnp.concatenate(ring(high, "dx"), axis=0)
    return place_rows(info, ring(along_z, "dx") + ring(along_x, "dz"), low.shape[1])


def pair_blocks(block, yh):
    other = send(block, route(dyh=1))
    return jnp.where(yh == 0, block, other), jnp.where(yh == 0, other, block)


def shards(hidden, qkv_first, wo_first, norm_gain, wqkv_second, wo_second, tile_clip, clip_frames):
    patch = lax.axis_index("patch")
    head = lax.axis_index("head")
    x, z, yh = patch // 8, patch // 2 % 4, patch % 2
    yl, c = head // 2, head % 2
    own_clip = tile_clip[patch]
    next_clip = tile_clip[(patch + 1) % NPATCH]
    info = jnp.stack(
        [
            c,
            yl,
            x,
            z,
            clip_frames[own_clip],
            clip_frames[next_clip],
            (own_clip == next_clip).astype(jnp.int32),
            yh,
        ]
    ).astype(jnp.int32)

    first_low, first_high = pair_blocks(wo_first, yh)
    weight_first = gather_rows(info, first_low, first_high)

    rest = jnp.concatenate(
        [wqkv_second[:, 0], wqkv_second[:, 1], wqkv_second[:, 2], wo_second], axis=1
    )
    rest_pair = jnp.concatenate(pair_blocks(rest, yh), axis=0)
    groups = [[(g * 2) + h for g in range(16)] for h in range(2)]
    weights = lax.all_gather(rest_pair, "patch", axis=0, tiled=True, axis_index_groups=groups)

    near, far = aligned_attention(info, qkv_first.reshape(3, 768, 640))
    near = send(near, tile_route(-1, 0))

    def hidden_half(cols):
        return jnp.roll(cols, -1, axis=0).reshape(4, 96, 640)

    hid_far = hidden_half(hidden[:, :, 8:])
    hid_near = send(hidden_half(hidden[:, :, :8]), tile_route(-1, 0))
    gain = norm_gain.reshape(1, 2560)

    parts = []
    for window in range(2):
        to_core, keep = project_first(info, window, far, near, weight_first, hid_far, hid_near)
        chip = keep + send(to_core, route(dc=1)).astype(F32)
        full = chip + send(chip.astype(BF16), route(dyl=1)).astype(F32)
        other = send(full.astype(BF16), route(dc=1))
        rows = shifted_attention(info, window, full, other, gain, weights)
        to_core, keep = project_second(info, rows, weights, full)
        recv = send(to_core, route(dc=1))
        own, to_pair, next_same, next_cross = split_rows(info, keep, recv)
        parts += [
            own,
            send(to_pair, route(dyl=1)),
            send(next_same, tile_route(1, 0)),
            send(next_cross, tile_route(1, 1)),
        ]
    return final_rows(parts)


def solution(mesh):
    in_specs = (
        P(None, None, "patch", "head"),
        P(None, None, None, "patch", "head"),
        P("patch", "head"),
        P(),
        P("patch", None, "head"),
        P("patch", "head"),
        P(),
        P(),
    )
    out_specs = P(None, None, "patch", "head")
    return jax.shard_map(shards, mesh=mesh, in_specs=in_specs, out_specs=out_specs, check_vma=False)
```

```python
import functools
import math

import jax
import jax.numpy as jnp
from jax import lax
from jax.experimental import pallas as pl
from jax.experimental.pallas import tpu as pltpu
from jax.sharding import PartitionSpec as P

HD = 128
EPSILON = 1e-06
MASKED_SCORE = -1e30
EXP2_SCALE = math.log2(math.e) / math.sqrt(HD)
BF16 = jnp.bfloat16
F32 = jnp.float32
AXES = ("patch", "head")
NX, NZ, NPATCH, NDEV = 4, 4, 32, 128
FIRST, LOW, HIGH, LAST = (0, 640), (640, 1024), (1664, 896), (2560, 640)
HALF = 1664
VMEM_MIB = {
    "join": 4,
    "aligned_attention": 12,
    "bundle_first": 6,
    "bundle_rest": 18,
    "project_first": 16,
    "shifted_attention": 34,
    "project_second": 16,
    "chip_sum": 5,
    "block_sum": 5,
    "near_rows": 6,
    "near_sum": 6,
    "far_rows": 6,
    "split_rows": 10,
    "final_rows": 6,
}
MODEL_US = {
    "join": 2,
    "aligned_attention": 6,
    "bundle_first": 2,
    "bundle_rest": 3,
    "project_first": 30,
    "shifted_attention": 10,
    "project_second": 6,
    "split_rows": 1,
    "final_rows": 3,
}
ANYWHERE = pl.BlockSpec(memory_space=pl.ANY)
SMALL = pl.BlockSpec(memory_space=pltpu.SMEM)


def coordinates():
    patch, head = lax.axis_index("patch"), lax.axis_index("head")
    return patch // 8, patch // 2 % 4, patch % 2, head // 2, head % 2


def device_of(x, z, yh, yl, c):
    return ((((x % NX) * NZ + z % NZ) * 2 + yh % 2) * 2 + yl % 2) * 2 + c % 2


def route(dyh=0, dyl=0, dc=0):
    pairs = []
    for i in range(NDEV):
        c, yl, yh, z, x = i % 2, i // 2 % 2, i // 4 % 2, i // 8 % 4, i // 32
        pairs.append((i, device_of(x, z, yh + dyh, yl + dyl, c + dc)))
    return pairs


def ring_route(stage, step):
    pairs = []
    for i in range(NDEV):
        c, yl, yh, z, x = i % 2, i // 2 % 2, i // 4 % 2, i // 8 % 4, i // 32
        dx, dz = (step, 0) if (c + stage) % 2 else (0, step)
        pairs.append((i, device_of(x + dx, z + dz, yh, yl, c)))
    return pairs


def tile_route(step, flip):
    return [(i, ((i + 4 * step) % NDEV) ^ (2 * flip)) for i in range(NDEV)]


def send(block, pairs):
    return lax.ppermute(block, AXES, pairs)


def call(kernel, name, out_shape, **more):
    return pl.pallas_call(
        kernel,
        out_shape=out_shape,
        compiler_params=pltpu.CompilerParams(vmem_limit_bytes=VMEM_MIB[name] << 20),
        cost_estimate=pl.CostEstimate(
            flops=1150000000 * MODEL_US[name], bytes_accessed=1024, transcendentals=0
        ),
        name=name,
        **more,
    )


def shape_of(shape, dtype=BF16):
    return jax.ShapeDtypeStruct(shape, dtype)


def join_kernel(first, middle, last, out):
    out[:, :640] = first[...]
    for n in range(3):
        out[:, 640 * n + 640 : 640 * n + 1280] = middle[n]
    out[:, 2560:] = last[...]


def bundle_kernel(cuts, *refs):
    x, z, yh, _, c = coordinates()
    position = jnp.where(c == 0, z, x)
    outs = refs[-len(cuts) :]
    for lane in range(2):
        own, ahead, behind, low, high = refs[5 * lane : 5 * lane + 5]
        row = (yh + lane) % 2
        for out, (lower, width) in zip(outs, cuts):
            cols = slice(lower, lower + width)
            out[position, row] = own[:, cols]
            out[(position + 1) % 4, row] = ahead[:, cols]
            out[(position + 3) % 4, row] = behind[:, cols]
            if lower < HALF:
                out[(position + 2) % 4, row] = low[:, cols]
            else:
                out[(position + 2) % 4, row] = high[:, lower - HALF : lower - HALF + width]


def bundles(pieces, cuts, block, name, after):
    specs = [pl.BlockSpec((80, min(block, piece.shape[1])), lambda i: (0, 0)) for piece in pieces]
    return call(
        functools.partial(bundle_kernel, cuts),
        name,
        [shape_of((4, 2, 80, width)) for _, width in cuts],
        grid=(1,),
        in_specs=specs + [ANYWHERE] * len(after),
        out_specs=[pl.BlockSpec((4, 2, 80, width), lambda i: (0, 0, 0, 0)) for _, width in cuts],
    )(*pieces, *after)


def ring_columns(block):
    ahead = send(block, ring_route(0, -1))
    behind = send(block, ring_route(0, 1))
    low = send(behind[:, :HALF], ring_route(0, 1))
    high = send(ahead[:, HALF:], ring_route(0, -1))
    return [block, ahead, behind, low, high]


def ring_slots(block):
    ahead = send(block, ring_route(1, -1))
    behind = send(block, ring_route(1, 1))
    low = send(behind[:2], ring_route(1, 1))
    high = send(ahead[2:], ring_route(1, -1))
    return [block, ahead, behind, low, high]


SLOTS = [(0, 0, 4), (1, 0, 4), (3, 0, 4), (2, 0, 2), (2, 2, 2)]


def ring_pair(low, high):
    low_behind = send(low, ring_route(1, 1))
    high_ahead = send(high, ring_route(1, -1))
    high_behind = send(high, ring_route(1, 1))
    low_ahead = send(low, ring_route(1, -1))
    low_across = send(low_behind, ring_route(1, 1))
    high_across = send(high_ahead, ring_route(1, -1))
    return [low, low_ahead, low_behind, low_across], [high, high_ahead, high_behind, high_across]


PAIR_SLOTS = [(0, 0, 4), (1, 0, 4), (3, 0, 4), (2, 0, 4)]


def place_start(pieces, slots, weight, sems):
    x, z, _, _, c = coordinates()

    @pl.when(c == 0)
    def _():
        for n, (piece, (k, lower, count)) in enumerate(zip(pieces, slots)):
            pltpu.make_async_copy(
                piece, weight.at[(x + k) % 4, pl.ds(lower, count)], sems.at[n]
            ).start()

    @pl.when(c == 1)
    def _():
        for n, (piece, (k, lower, count)) in enumerate(zip(pieces, slots)):
            pltpu.make_async_copy(
                piece, weight.at[pl.ds(lower, count), (z + k) % 4], sems.at[n]
            ).start()


def place_wait(pieces, slots, weight, sems):
    for n, (piece, (_, lower, count)) in enumerate(zip(pieces, slots)):
        pltpu.make_async_copy(piece, weight.at[0, pl.ds(lower, count)], sems.at[n]).wait()


def softmax_values(scores, values):
    top = jnp.max(scores, axis=-1, keepdims=True)
    lifted = jnp.exp2((scores - top) * EXP2_SCALE)
    total = jnp.sum(lifted, axis=-1, keepdims=True)
    context = jnp.dot(lifted.astype(BF16), values, preferred_element_type=F32)
    return context / total


def scores_of(query, key):
    return lax.dot_general(query, key, (((1,), (1,)), ((), ())), preferred_element_type=F32)


def aligned_kernel(tile_clip, clip_frames, qkv, hidden, out_far, out_near):
    frames_own = clip_frames[tile_clip[lax.axis_index("patch")]]
    lane = lax.broadcasted_iota(jnp.int32, (1, 384), 1) // 192
    row = lax.broadcasted_iota(jnp.int32, (384, 1), 0) // 192

    def put(place, frame):
        out_near[place] = frame[:, :8].reshape(96, HD).astype(BF16)
        out_far[place] = frame[:, 8:].reshape(96, HD).astype(BF16)

    for window in range(2):
        rows = slice(window * 384, window * 384 + 384)
        scores = scores_of(qkv[0, rows], qkv[1, rows])
        scores = jnp.where(2 * window + lane < frames_own, scores, MASKED_SCORE)
        context = softmax_values(scores, qkv[2, rows])
        context = jnp.where(2 * window + row < frames_own, context, 0.0)
        context = context.reshape(2, 12, 16, HD)
        for half in range(2):
            frame = 2 * window + half
            put((frame + 3) % 4, context[half])
            put(4 + (frame + 3) % 4, hidden[frame].astype(F32))


def aligned_attention(tile_clip, clip_frames, qkv, hidden):
    spec = pl.BlockSpec((8, 96, HD), lambda j: (0, 0, j))
    return call(
        aligned_kernel,
        "aligned_attention",
        [shape_of((8, 96, 640))] * 2,
        grid=(5,),
        in_specs=[
            SMALL,
            SMALL,
            pl.BlockSpec((3, 768, HD), lambda j: (0, 0, j)),
            pl.BlockSpec((4, 12, 16, HD), lambda j: (0, 0, 0, j)),
        ],
        out_specs=[spec, spec],
    )(tile_clip, clip_frames, qkv, hidden)


def shifted_kernel(window, tile_clip, clip_frames, own, other, gain, *refs):
    pieces, (out, normed, qkv, low, high, sems) = refs[:8], refs[-6:]
    c = coordinates()[4]
    place_start(pieces[:4], PAIR_SLOTS, low, sems.at[0])
    place_start(pieces[4:], PAIR_SLOTS, high, sems.at[1])
    patch = lax.axis_index("patch")
    clip_own, clip_next = tile_clip[patch], tile_clip[(patch + 1) % NPATCH]
    frames_own, frames_next = clip_frames[clip_own], clip_frames[clip_next]

    mine = own[...]
    theirs = other[...].astype(F32)
    squares = jnp.sum(mine * mine, axis=-1, keepdims=True) + jnp.sum(
        theirs * theirs, axis=-1, keepdims=True
    )
    scale = lax.rsqrt(squares * (1.0 / 2560) + EPSILON)
    for a in range(2):
        for source, core in ((mine, c), (theirs, 1 - c)):
            lower = pl.multiple_of((2 * a + core) * 640, 128)
            part = source[:, a * 640 : (a + 1) * 640] * scale * gain[:, pl.ds(lower, 640)]
            normed[:, pl.ds(lower, 640)] = part.astype(BF16)

    def project(weight, width):
        return jnp.dot(
            normed[...], weight[...].reshape(2560, width), preferred_element_type=F32
        ).astype(BF16)

    place_wait(pieces[:4], PAIR_SLOTS, low, sems.at[0])
    qkv[:, :1024] = project(low, 1024)
    place_wait(pieces[4:], PAIR_SLOTS, high, sems.at[1])
    qkv[:, 1024:] = project(high, 896)

    first, second = ((1, 2), (3, 0))[window]
    lane = lax.broadcasted_iota(jnp.int32, (1, 384), 1)
    row = lax.broadcasted_iota(jnp.int32, (384, 1), 0)

    def live(position):
        frame = jnp.where(position // 96 % 2 == 0, first, second)
        return frame < jnp.where(position < 192, frames_own, frames_next)

    alike = ((lane < 192) == (row < 192)) | (clip_own == clip_next)
    allowed = alike & live(lane)
    live_rows = live(row)
    for head in range(5):
        query, key, value = [
            qkv[:, 640 * n + head * HD : 640 * n + head * HD + HD] for n in range(3)
        ]
        scores = jnp.where(allowed, scores_of(query, key), MASKED_SCORE)
        context = softmax_values(scores, value)
        out[:, head * HD : head * HD + HD] = jnp.where(live_rows, context, 0.0).astype(BF16)


def shifted_attention(window, tile_clip, clip_frames, own, other, gain, pieces, after):
    def whole(shape):
        return pl.BlockSpec(shape, lambda i: (0, 0))

    return call(
        functools.partial(shifted_kernel, window),
        "shifted_attention",
        shape_of((384, 640)),
        grid=(1,),
        in_specs=[SMALL, SMALL, whole((384, 1280)), whole((384, 1280)), whole((1, 2560))]
        + [ANYWHERE] * (8 + len(after)),
        out_specs=whole((384, 640)),
        scratch_shapes=[
            pltpu.VMEM((384, 2560), BF16),
            pltpu.VMEM((384, 1920), BF16),
            pltpu.VMEM((4, 4, 2, 80, LOW[1]), BF16),
            pltpu.VMEM((4, 4, 2, 80, HIGH[1]), BF16),
            pltpu.SemaphoreType.DMA((2, 4)),
        ],
    )(tile_clip, clip_frames, own, other, gain, *pieces, *after)


def project_rows(rows, pieces, extra, out_send, out_keep, weight, sems):
    _, _, _, yl, c = coordinates()
    place_start(pieces, SLOTS, weight, sems)
    place_wait(pieces, SLOTS, weight, sems)

    def part(block):
        return lax.dot_general(
            rows,
            weight[block].reshape(640, 640),
            (((1,), (1,)), ((), ())),
            preferred_element_type=F32,
        )

    for a in range(2):
        cols = slice(640 * a, 640 * a + 640)
        out_send[:, cols] = part(2 * a + 1 - c).astype(BF16)
        out_keep[:, cols] = part(2 * a + c)
    mine = pl.ds(pl.multiple_of(yl * 640, 128), 640)
    out_keep[:, mine] += extra


def project_first_kernel(far, near, hid_far, hid_near, *refs):
    def rows(first, second):
        return jnp.concatenate(
            [first[...].reshape(192, 640), second[...].reshape(192, 640)], axis=0
        )

    extra = rows(hid_far, hid_near).astype(F32)
    project_rows(rows(far, near), refs[:5], extra, *refs[-4:])


def project_second_kernel(rows, full, *refs):
    yl = coordinates()[3]
    mine = pl.ds(pl.multiple_of(yl * 640, 128), 640)
    project_rows(rows[...], refs[:5], full[:, mine], *refs[-4:])


def project_call(kernel, name, operands, specs, pieces, after):
    return call(
        kernel,
        name,
        [shape_of((384, 1280)), shape_of((384, 1280), F32)],
        grid=(1,),
        in_specs=specs + [ANYWHERE] * (5 + len(after)),
        out_specs=[pl.BlockSpec((384, 1280), lambda i: (0, 0))] * 2,
        scratch_shapes=[pltpu.VMEM((4, 4, 2, 80, 640), BF16), pltpu.SemaphoreType.DMA((5,))],
    )(*operands, *pieces, *after)


def project_first(window, far, near, pieces, after):
    context = pl.BlockSpec((2, 96, 640), lambda i: (window, 0, 0))
    hidden = pl.BlockSpec((2, 96, 640), lambda i: (2 + window, 0, 0))
    specs = [context, context, hidden, hidden]
    operands = (far, near, far, near)
    return project_call(project_first_kernel, "project_first", operands, specs, pieces, after)


def project_second(rows, full, pieces, after):
    specs = [
        pl.BlockSpec((384, 640), lambda i: (0, 0)),
        pl.BlockSpec((384, 1280), lambda i: (0, 0)),
    ]
    return project_call(project_second_kernel, "project_second", (rows, full), specs, pieces, after)


def split_kernel(keep, recv, own, to_pair, next_same, next_cross):
    yl = coordinates()[3]

    def total(block):
        cols = pl.ds(pl.multiple_of(block * 640, 128), 640)
        return keep[:, cols] + recv[:, cols].astype(F32)

    mine, pair = total(yl), total(1 - yl)
    own[...] = mine[:192]
    to_pair[...] = pair[:192].astype(BF16)
    next_same[...] = mine[192:].astype(BF16)
    next_cross[...] = pair[192:].astype(BF16)


def split_rows(keep, recv):
    out = shape_of((192, 640))
    return call(split_kernel, "split_rows", [shape_of((192, 640), F32), out, out, out])(keep, recv)


def final_kernel(*refs):
    out = refs[-1]
    for window in range(2):
        own, pair, same, cross = [ref[...] for ref in refs[4 * window : 4 * window + 4]]
        far = (own + pair.astype(F32)).reshape(2, 12, 8, HD)
        near = (same.astype(F32) + cross.astype(F32)).reshape(2, 12, 8, HD)
        for half in range(2):
            out[(2 * window + half + 1) % 4] = jnp.concatenate([near[half], far[half]], axis=1)


def final_rows(operands):
    return call(
        final_kernel,
        "final_rows",
        shape_of((4, 12, 16, 640), F32),
        grid=(5,),
        in_specs=[pl.BlockSpec((192, HD), lambda j: (0, j))] * 8,
        out_specs=pl.BlockSpec((4, 12, 16, HD), lambda j: (0, 0, 0, j)),
    )(*operands)


def shards(hidden, qkv_first, wo_first, norm_gain, wqkv_second, wo_second, tile_clip, clip_frames):
    blocks = call(join_kernel, "join", shape_of((80, 3200)))(
        wo_first, jnp.transpose(wqkv_second, (1, 0, 2)), wo_second
    )
    partner = send(blocks, route(dyh=1))
    far, near = aligned_attention(tile_clip, clip_frames, qkv_first.reshape(3, 768, 640), hidden)
    near = send(near, tile_route(-1, 0))
    rings = ring_columns(blocks) + ring_columns(partner)
    (bundle,) = bundles(rings, [FIRST], 640, "bundle_first", [])
    first = ring_slots(bundle)
    low, high, bundle = bundles(rings, [LOW, HIGH, LAST], 3200, "bundle_rest", [])
    rest = [low, high, bundle]
    low, high = ring_pair(low, high)
    last = ring_slots(bundle)
    gain = norm_gain.reshape(1, 2560)

    parts, gates = [], []
    for window in range(2):
        to_core, keep = project_first(window, far, near, first, [])
        chip = keep + send(to_core, route(dc=1)).astype(F32)
        full = chip + send(chip.astype(BF16), route(dyl=1)).astype(F32)
        other = send(full.astype(BF16), route(dc=1))
        rows = shifted_attention(
            window, tile_clip, clip_frames, full, other, gain, low + high, gates
        )
        to_core, keep = project_second(rows, full, last, [])
        own, to_pair, next_same, next_cross = split_rows(keep, send(to_core, route(dc=1)))
        gates = [to_pair]
        parts += [
            own,
            send(to_pair, route(dyl=1)),
            send(next_same, tile_route(1, 0)),
            send(next_cross, tile_route(1, 1)),
        ]
    return final_rows(parts)


def solution(mesh):
    in_specs = (
        P(None, None, "patch", "head"),
        P(None, None, None, "patch", "head"),
        P("patch", "head"),
        P(),
        P("patch", None, "head"),
        P("patch", "head"),
        P(),
        P(),
    )
    out_specs = P(None, None, "patch", "head")
    return jax.shard_map(shards, mesh=mesh, in_specs=in_specs, out_specs=out_specs, check_vma=False)
```

```python
import functools
import math

import jax
import jax.numpy as jnp
from jax import lax
from jax.experimental import pallas as pl
from jax.experimental.pallas import tpu as pltpu
from jax.sharding import PartitionSpec as P

HD = 128
EPSILON = 1e-06
MASKED_SCORE = -1e30
EXP2_SCALE = math.log2(math.e) / math.sqrt(HD)
BF16 = jnp.bfloat16
F32 = jnp.float32
AXES = ("patch", "head")
NX, NZ, NPATCH, NDEV = 4, 4, 32, 128
FIRST, MIDDLE, LAST = (0, 640), (640, 1920), (2560, 640)
HALF = 1664
VMEM_MIB = {
    "join": 4,
    "aligned_attention": 12,
    "bundle_first": 6,
    "hidden_halves": 4,
    "bundle_rest": 18,
    "halves": 6,
    "project_first": 16,
    "shifted_attention": 40,
    "project_second": 16,
    "chip_sum": 5,
    "block_sum": 5,
    "near_rows": 6,
    "near_sum": 6,
    "far_rows": 6,
    "final_rows": 6,
}
MODEL_US = {
    "join": 2,
    "aligned_attention": 6,
    "bundle_first": 2,
    "hidden_halves": 2,
    "bundle_rest": 3,
    "halves": 1,
    "project_first": 30,
    "shifted_attention": 18,
    "project_second": 6,
    "chip_sum": 2,
    "block_sum": 2,
    "near_rows": 1,
    "near_sum": 1,
    "far_rows": 1,
    "final_rows": 3,
}
ANYWHERE = pl.BlockSpec(memory_space=pl.ANY)
INSIDE = pl.BlockSpec(memory_space=pltpu.VMEM)
SMALL = pl.BlockSpec(memory_space=pltpu.SMEM)


def coordinates():
    patch, head = lax.axis_index("patch"), lax.axis_index("head")
    return patch // 8, patch // 2 % 4, patch % 2, head // 2, head % 2


def device_of(x, z, yh, yl, c):
    return ((((x % NX) * NZ + z % NZ) * 2 + yh % 2) * 2 + yl % 2) * 2 + c % 2


def route(dyh=0, dyl=0, dc=0):
    pairs = []
    for i in range(NDEV):
        c, yl, yh, z, x = i % 2, i // 2 % 2, i // 4 % 2, i // 8 % 4, i // 32
        pairs.append((i, device_of(x, z, yh + dyh, yl + dyl, c + dc)))
    return pairs


def ring_route(stage, step):
    pairs = []
    for i in range(NDEV):
        c, yl, yh, z, x = i % 2, i // 2 % 2, i // 4 % 2, i // 8 % 4, i // 32
        dx, dz = (step, 0) if (c + stage) % 2 else (0, step)
        pairs.append((i, device_of(x + dx, z + dz, yh, yl, c)))
    return pairs


def tile_route(step, flip):
    return [(i, ((i + 4 * step) % NDEV) ^ (2 * flip)) for i in range(NDEV)]


def send(block, pairs):
    return lax.ppermute(block, AXES, pairs)


def call(kernel, name, out_shape, **more):
    return pl.pallas_call(
        kernel,
        out_shape=out_shape,
        compiler_params=pltpu.CompilerParams(vmem_limit_bytes=VMEM_MIB[name] << 20),
        cost_estimate=pl.CostEstimate(
            flops=1150000000 * MODEL_US[name], bytes_accessed=1024, transcendentals=0
        ),
        name=name,
        **more,
    )


def shape_of(shape, dtype=BF16):
    return jax.ShapeDtypeStruct(shape, dtype)


def join_kernel(first, middle, last, out):
    out[:, :640] = first[...]
    for n in range(3):
        out[:, 640 * n + 640 : 640 * n + 1280] = middle[n]
    out[:, 2560:] = last[...]


def bundle_kernel(cuts, *refs):
    x, z, yh, _, c = coordinates()
    position = jnp.where(c == 0, z, x)
    outs = refs[-len(cuts) :]
    for lane in range(2):
        own, ahead, behind, low, high = refs[5 * lane : 5 * lane + 5]
        row = (yh + lane) % 2
        for out, (lower, width) in zip(outs, cuts):
            cols = slice(lower, lower + width)
            out[position, row] = own[:, cols]
            out[(position + 1) % 4, row] = ahead[:, cols]
            out[(position + 3) % 4, row] = behind[:, cols]
            split = min(max(HALF - lower, 0), width)
            if split > 0:
                out[(position + 2) % 4, row, :, :split] = low[:, lower : lower + split]
            if split < width:
                start = lower + split - HALF
                out[(position + 2) % 4, row, :, split:] = high[:, start : start + width - split]


def bundles(pieces, cuts, block, name, after):
    specs = [pl.BlockSpec((80, min(block, piece.shape[1])), lambda i: (0, 0)) for piece in pieces]
    return call(
        functools.partial(bundle_kernel, cuts),
        name,
        [shape_of((4, 2, 80, width)) for _, width in cuts],
        grid=(1,),
        in_specs=specs + [ANYWHERE] * len(after),
        out_specs=[pl.BlockSpec((4, 2, 80, width), lambda i: (0, 0, 0, 0)) for _, width in cuts],
    )(*pieces, *after)


def ring_columns(block):
    ahead = send(block, ring_route(0, -1))
    behind = send(block, ring_route(0, 1))
    low = send(behind[:, :HALF], ring_route(0, 1))
    high = send(ahead[:, HALF:], ring_route(0, -1))
    return [block, ahead, behind, low, high]


def ring_direct(block):
    return [block] + [send(block, ring_route(1, step)) for step in (-1, 2, 1)]


DIRECT_SLOTS = [(0, 0, 4), (1, 0, 4), (2, 0, 4), (3, 0, 4)]
SLOTS = [(0, 0, 4), (1, 0, 4), (3, 0, 4), (2, 0, 2), (2, 2, 2)]


def halves_kernel(behind, ahead, last, out_low, out_high, out_last):
    out_low[...] = behind[...]
    out_high[...] = ahead[...]
    out_last[...] = last[...]


def ring_forward(block, last):
    ahead = send(block, ring_route(1, -1))
    behind = send(block, ring_route(1, 1))

    def part(shape, index):
        return pl.BlockSpec(shape, index)

    one, two = (1, 1, 80, 1920), (1, 2, 80, 640)
    low, high, last = call(
        halves_kernel,
        "halves",
        [shape_of((2, 2, 80, 1920))] * 2 + [shape_of(last.shape)],
        grid=(4,),
        in_specs=[
            part(one, lambda i: (i // 2, i % 2, 0, 0)),
            part(one, lambda i: (2 + i // 2, i % 2, 0, 0)),
            part(two, lambda i: (i, 0, 0, 0)),
        ],
        out_specs=[
            part(one, lambda i: (i // 2, i % 2, 0, 0)),
            part(one, lambda i: (i // 2, i % 2, 0, 0)),
            part(two, lambda i: (i, 0, 0, 0)),
        ],
    )(behind, ahead, last)
    halves = [low, high]
    low = send(low, ring_route(1, 1))
    high = send(high, ring_route(1, -1))
    return [block, ahead, behind, low, high], last, halves


def place_start(pieces, slots, lower_col, weight, sems):
    x, z, _, _, c = coordinates()
    width = weight.shape[-1]

    def start(where):
        for n, (piece, (k, lower, count)) in enumerate(zip(pieces, slots)):
            source = piece
            if piece.shape[-1] != width:
                source = piece.at[:, :, :, pl.ds(lower_col, width)]
            target = weight.at[where(k, pl.ds(lower, count))]
            pltpu.make_async_copy(source, target, sems.at[n]).start()

    @pl.when(c == 0)
    def _():
        start(lambda k, rows: ((x + k) % 4, rows))

    @pl.when(c == 1)
    def _():
        start(lambda k, rows: (rows, (z + k) % 4))


def place_wait(slots, weight, sems):
    for n, (_, lower, count) in enumerate(slots):
        target = weight.at[0, pl.ds(lower, count)]
        pltpu.make_async_copy(target, target, sems.at[n]).wait()


def softmax_values(scores, values):
    top = jnp.max(scores, axis=-1, keepdims=True)
    lifted = jnp.exp2((scores - top) * EXP2_SCALE)
    total = jnp.sum(lifted, axis=-1, keepdims=True)
    context = jnp.dot(lifted.astype(BF16), values, preferred_element_type=F32)
    return context / total


def scores_of(query, key):
    return lax.dot_general(query, key, (((1,), (1,)), ((), ())), preferred_element_type=F32)


def aligned_kernel(tile_clip, clip_frames, qkv, hidden, out_far, out_near):
    frames_own = clip_frames[tile_clip[lax.axis_index("patch")]]
    lane = lax.broadcasted_iota(jnp.int32, (1, 384), 1) // 192
    row = lax.broadcasted_iota(jnp.int32, (384, 1), 0) // 192

    def put(place, frame):
        out_near[place] = frame[:, :8].reshape(96, HD).astype(BF16)
        out_far[place] = frame[:, 8:].reshape(96, HD).astype(BF16)

    for window in range(2):
        rows = slice(window * 384, window * 384 + 384)
        scores = scores_of(qkv[0, rows], qkv[1, rows])
        scores = jnp.where(2 * window + lane < frames_own, scores, MASKED_SCORE)
        context = softmax_values(scores, qkv[2, rows])
        context = jnp.where(2 * window + row < frames_own, context, 0.0)
        context = context.reshape(2, 12, 16, HD)
        for half in range(2):
            frame = 2 * window + half
            put((frame + 3) % 4, context[half])
            put(4 + (frame + 3) % 4, hidden[frame].astype(F32))


def aligned_attention(tile_clip, clip_frames, qkv, hidden):
    spec = pl.BlockSpec((8, 96, HD), lambda j: (0, 0, j))
    return call(
        aligned_kernel,
        "aligned_attention",
        [shape_of((8, 96, 640))] * 2,
        grid=(5,),
        in_specs=[
            SMALL,
            SMALL,
            pl.BlockSpec((3, 768, HD), lambda j: (0, 0, j)),
            pl.BlockSpec((4, 12, 16, HD), lambda j: (0, 0, 0, j)),
        ],
        out_specs=[spec, spec],
    )(tile_clip, clip_frames, qkv, hidden)


def shifted_kernel(
    tile_clip, clip_frames, own_far, own_near, other_far, other_near, gain, *refs
):
    pieces, (out, normed, qkv, low, high, sems) = refs[:5], refs[-6:]
    c = coordinates()[4]
    place_start(pieces, SLOTS, 0, low, sems.at[0])
    place_start(pieces, SLOTS, 1024, high, sems.at[1])
    patch = lax.axis_index("patch")
    clip_own, clip_next = tile_clip[patch], tile_clip[(patch + 1) % NPATCH]
    frames_own, frames_next = clip_frames[clip_own], clip_frames[clip_next]

    for half, (own, other) in enumerate(((own_far, other_far), (own_near, other_near))):
        rows = slice(384 * half, 384 * half + 384)
        mine, theirs = own[...].astype(F32), other[...].astype(F32)
        squares = jnp.sum(mine * mine, axis=-1, keepdims=True) + jnp.sum(
            theirs * theirs, axis=-1, keepdims=True
        )
        scale = lax.rsqrt(squares * (1.0 / 2560) + EPSILON)
        for a in range(2):
            for source, core in ((mine, c), (theirs, 1 - c)):
                lower = pl.multiple_of((2 * a + core) * 640, 128)
                part = source[:, a * 640 : (a + 1) * 640] * scale * gain[:, pl.ds(lower, 640)]
                normed[rows, pl.ds(lower, 640)] = part.astype(BF16)

    def project(weight, width):
        return jnp.dot(
            normed[...], weight[...].reshape(2560, width), preferred_element_type=F32
        ).astype(BF16)

    place_wait(SLOTS, low, sems.at[0])
    qkv[:, :1024] = project(low, 1024)
    place_wait(SLOTS, high, sems.at[1])
    qkv[:, 1024:] = project(high, 896)

    lane = lax.broadcasted_iota(jnp.int32, (1, 384), 1)
    row = lax.broadcasted_iota(jnp.int32, (384, 1), 0)
    alike = ((lane < 192) == (row < 192)) | (clip_own == clip_next)
    for window in range(2):
        first, second = ((1, 2), (3, 0))[window]
        far = slice(192 * window, 192 * window + 192)
        near = slice(384 + 192 * window, 384 + 192 * window + 192)

        def live(position):
            frame = jnp.where(position // 96 % 2 == 0, first, second)
            return frame < jnp.where(position < 192, frames_own, frames_next)

        allowed = alike & live(lane)
        live_rows = live(row)
        for head in range(5):
            query, key, value = [
                jnp.concatenate([qkv[far, cols], qkv[near, cols]], axis=0)
                for cols in [
                    slice(640 * n + head * HD, 640 * n + head * HD + HD) for n in range(3)
                ]
            ]
            scores = jnp.where(allowed, scores_of(query, key), MASKED_SCORE)
            context = softmax_values(scores, value)
            context = jnp.where(live_rows, context, 0.0).astype(BF16)
            cols = slice(head * HD, head * HD + HD)
            out[far, cols] = context[:192]
            out[near, cols] = context[192:]


def shifted_attention(tile_clip, clip_frames, blocks, gain, pieces):
    return call(
        shifted_kernel,
        "shifted_attention",
        shape_of((768, 640)),
        in_specs=[SMALL, SMALL] + [INSIDE] * 5 + [ANYWHERE] * 5,
        scratch_shapes=[
            pltpu.VMEM((768, 2560), BF16),
            pltpu.VMEM((768, 1920), BF16),
            pltpu.VMEM((4, 4, 2, 80, 1024), BF16),
            pltpu.VMEM((4, 4, 2, 80, 896), BF16),
            pltpu.SemaphoreType.DMA((2, 5)),
        ],
    )(tile_clip, clip_frames, *blocks, gain, *pieces)


def project_rows(rows, pieces, extra, out_send, out_keep, weight, sems):
    _, _, _, yl, c = coordinates()
    i = pl.program_id(0)

    @pl.when(i == 0)
    def _():
        place_start(pieces, DIRECT_SLOTS, 0, weight, sems)
        place_wait(DIRECT_SLOTS, weight, sems)

    part = lax.dot_general(
        rows[...].reshape(384, 640),
        weight[2 * (i % 2) + jnp.where(i < 2, 1 - c, c)].reshape(640, 640),
        (((1,), (1,)), ((), ())),
        preferred_element_type=F32,
    )

    @pl.when(i < 2)
    def _():
        out_send[...] = part.astype(BF16)

    @pl.when(i - 2 == yl)
    def _():
        out_keep[...] = (part + extra().astype(F32)).astype(BF16)

    @pl.when((i >= 2) & (i - 2 != yl))
    def _():
        out_keep[...] = part.astype(BF16)


def project_first_kernel(rows, hidden, *refs):
    project_rows(rows, refs[:4], lambda: hidden[...].reshape(384, 640), *refs[-4:])


def project_second_kernel(rows, full, *refs):
    def extra():
        return full[:, pl.ds(pl.multiple_of(coordinates()[3] * 640, 128), 640)]

    project_rows(rows, refs[:4], extra, *refs[-4:])


def project(kernel, name, operands, specs, pieces, after):
    return call(
        kernel,
        name,
        [shape_of((384, 1280))] * 2,
        grid=(4,),
        in_specs=specs + [ANYWHERE] * (len(pieces) + len(after)),
        out_specs=[
            pl.BlockSpec((384, 640), lambda i: (0, jnp.minimum(i, 1))),
            pl.BlockSpec((384, 640), lambda i: (0, jnp.maximum(i - 2, 0))),
        ],
        scratch_shapes=[pltpu.VMEM((4, 4, 2, 80, 640), BF16), pltpu.SemaphoreType.DMA((4,))],
    )(*operands, *pieces, *after)


def project_first(side, pieces, after):
    specs = [pl.BlockSpec((4, 96, 640), lambda i, n=n: (n, 0, 0)) for n in range(2)]
    return project(project_first_kernel, "project_first", (side, side), specs, pieces, after)


def project_second(side, rows, full, pieces, after):
    specs = [
        pl.BlockSpec((384, 640), lambda i: (side, 0)),
        pl.BlockSpec((384, 1280), lambda i: (0, 0)),
    ]
    return project(project_second_kernel, "project_second", (rows, full), specs, pieces, after)


def sum_kernel(count, *refs):
    refs[-1][...] = sum(ref[...].astype(F32) for ref in refs[:count]).astype(BF16)


def sums(name, terms, after):
    spec = pl.BlockSpec((128, 1280), lambda i: (i, 0))
    return call(
        functools.partial(sum_kernel, len(terms)),
        name,
        shape_of((384, 1280)),
        grid=(3,),
        in_specs=[spec] * len(terms) + [ANYWHERE] * len(after),
        out_specs=spec,
    )(*terms, *after)


def blocks_of(yl):
    return [pl.ds(pl.multiple_of(block * 640, 128), 640) for block in (yl, 1 - yl)]


def near_rows_kernel(keep, recv, *outs):
    mine, _ = blocks_of(coordinates()[3])
    for n, out in enumerate(outs):
        rows = slice(192 * n, 192 * n + 192)
        out[...] = (keep[rows, mine].astype(F32) + recv[rows, mine].astype(F32)).astype(BF16)


def near_sum_kernel(n, keep, recv, pair, out):
    _, other = blocks_of(coordinates()[3])
    rows = slice(192 * n, 192 * n + 192)
    total = keep[rows, other].astype(F32) + recv[rows, other].astype(F32)
    out[...] = (total + pair[...].astype(F32)).astype(BF16)


def far_rows_kernel(keep, recv, own, to_pair):
    mine, other = blocks_of(coordinates()[3])
    own[...] = keep[:, mine].astype(F32) + recv[:, mine].astype(F32)
    to_pair[...] = (keep[:, other].astype(F32) + recv[:, other].astype(F32)).astype(BF16)


def final_kernel(own, pair, near_0, near_1, out):
    i = pl.program_id(0)
    far = (own[...] + pair[...].astype(F32)).reshape(12, 8, 640)
    near = jnp.where(i < 2, near_0[...].astype(F32), near_1[...].astype(F32))
    out[0] = jnp.concatenate([near.reshape(12, 8, 640), far], axis=1)


def final_rows(*operands):
    rows = pl.BlockSpec((96, 640), lambda i: (i, 0))
    return call(
        final_kernel,
        "final_rows",
        shape_of((4, 12, 16, 640), F32),
        grid=(4,),
        in_specs=[
            rows,
            rows,
            pl.BlockSpec((96, 640), lambda i: (jnp.minimum(i, 1), 0)),
            pl.BlockSpec((96, 640), lambda i: (jnp.maximum(i - 2, 0), 0)),
        ],
        out_specs=pl.BlockSpec((1, 12, 16, 640), lambda i: ((i + 1) % 4, 0, 0, 0)),
    )(*operands)


def shards(hidden, qkv_first, wo_first, norm_gain, wqkv_second, wo_second, tile_clip, clip_frames):
    blocks = call(join_kernel, "join", shape_of((80, 3200)))(
        wo_first, jnp.transpose(wqkv_second, (1, 0, 2)), wo_second
    )
    partner = send(blocks, route(dyh=1))
    far, near = aligned_attention(tile_clip, clip_frames, qkv_first.reshape(3, 768, 640), hidden)
    near = send(near, tile_route(-1, 0))
    rings = ring_columns(blocks) + ring_columns(partner)
    (bundle,) = bundles(rings, [FIRST], 640, "bundle_first", [])
    first = ring_direct(bundle)
    middle, last = bundles(rings, [MIDDLE, LAST], 3200, "bundle_rest", [])
    middle, last, halves = ring_forward(middle, last)
    last = ring_direct(last)
    gain = norm_gain.reshape(1, 2560)

    fulls, chip, pair = [], [], []
    for side in (far, near):
        last_side = side is near
        to_core, keep = project_first(side, first, [chip] if last_side else [])
        recv = send(to_core, route(dc=1))
        chip = sums("chip_sum", [keep, recv], [] if last_side else [near])
        pair = send(chip, route(dyl=1))
        fulls.append(sums("block_sum", [chip, pair], [] if last_side else halves))
    blocks = fulls + [send(full, route(dc=1)) for full in fulls]
    rows = shifted_attention(tile_clip, clip_frames, blocks, gain, middle)

    low_rows = shape_of((384, 640))
    to_core, near_keep = project_second(1, rows, fulls[1], last, [])
    near_recv = send(to_core, route(dc=1))
    half_rows = shape_of((192, 640))
    pairs = call(near_rows_kernel, "near_rows", [half_rows] * 2)(near_keep, near_recv)
    to_core, keep = project_second(0, rows, fulls[0], last, [])
    own, pair_far = call(far_rows_kernel, "far_rows", [shape_of((384, 640), F32), low_rows])(
        keep, send(to_core, route(dc=1))
    )
    nears = []
    for n, pair in enumerate(pairs):
        total = call(functools.partial(near_sum_kernel, n), "near_sum", half_rows)(
            near_keep, near_recv, send(pair, route(dyl=1))
        )
        nears.append(send(total, tile_route(1, 1)))
    return final_rows(own, send(pair_far, route(dyl=1)), *nears)


def solution(mesh):
    in_specs = (
        P(None, None, "patch", "head"),
        P(None, None, None, "patch", "head"),
        P("patch", "head"),
        P(),
        P("patch", None, "head"),
        P("patch", "head"),
        P(),
        P(),
    )
    out_specs = P(None, None, "patch", "head")
    return jax.shard_map(shards, mesh=mesh, in_specs=in_specs, out_specs=out_specs, check_vma=False)
```

```python
import functools
import math

import jax
import jax.numpy as jnp
from jax import lax
from jax.experimental import pallas as pl
from jax.experimental.pallas import tpu as pltpu
from jax.sharding import PartitionSpec as P

HD = 128
EPSILON = 1e-06
MASKED_SCORE = -1e30
EXP2_SCALE = math.log2(math.e) / math.sqrt(HD)
BF16 = jnp.bfloat16
F32 = jnp.float32
AXES = ("patch", "head")
NX, NZ, NPATCH, NDEV = 4, 4, 32, 128
FIRST, MIDDLE, LAST = (0, 640), (640, 1920), (2560, 640)
HALF = 1664
VMEM_MIB = {
    "join": 4,
    "aligned_attention": 12,
    "bundle_first": 6,
    "hidden_halves": 4,
    "bundle_rest": 18,
    "halves": 6,
    "project_first": 16,
    "shifted_attention": 40,
    "project_second": 16,
    "chip_sum": 5,
    "block_sum": 5,
    "near_rows": 6,
    "near_sum": 6,
    "far_rows": 6,
    "final_rows": 6,
}
MODEL_US = {
    "join": 2,
    "aligned_attention": 6,
    "bundle_first": 2,
    "hidden_halves": 2,
    "bundle_rest": 3,
    "halves": 1,
    "project_first": 30,
    "shifted_attention": 10,
    "project_second": 6,
    "chip_sum": 2,
    "block_sum": 2,
    "near_rows": 1,
    "near_sum": 1,
    "far_rows": 1,
    "final_rows": 3,
}
ANYWHERE = pl.BlockSpec(memory_space=pl.ANY)
INSIDE = pl.BlockSpec(memory_space=pltpu.VMEM)
SMALL = pl.BlockSpec(memory_space=pltpu.SMEM)


def coordinates():
    patch, head = lax.axis_index("patch"), lax.axis_index("head")
    return patch // 8, patch // 2 % 4, patch % 2, head // 2, head % 2


def device_of(x, z, yh, yl, c):
    return ((((x % NX) * NZ + z % NZ) * 2 + yh % 2) * 2 + yl % 2) * 2 + c % 2


def route(dyh=0, dyl=0, dc=0):
    pairs = []
    for i in range(NDEV):
        c, yl, yh, z, x = i % 2, i // 2 % 2, i // 4 % 2, i // 8 % 4, i // 32
        pairs.append((i, device_of(x, z, yh + dyh, yl + dyl, c + dc)))
    return pairs


def ring_route(stage, step):
    pairs = []
    for i in range(NDEV):
        c, yl, yh, z, x = i % 2, i // 2 % 2, i // 4 % 2, i // 8 % 4, i // 32
        dx, dz = (step, 0) if (c + stage) % 2 else (0, step)
        pairs.append((i, device_of(x + dx, z + dz, yh, yl, c)))
    return pairs


def tile_route(step, flip):
    return [(i, ((i + 4 * step) % NDEV) ^ (2 * flip)) for i in range(NDEV)]


def send(block, pairs):
    return lax.ppermute(block, AXES, pairs)


def call(kernel, name, out_shape, **more):
    return pl.pallas_call(
        kernel,
        out_shape=out_shape,
        compiler_params=pltpu.CompilerParams(vmem_limit_bytes=VMEM_MIB[name] << 20),
        cost_estimate=pl.CostEstimate(
            flops=1150000000 * MODEL_US[name], bytes_accessed=1024, transcendentals=0
        ),
        name=name,
        **more,
    )


def shape_of(shape, dtype=BF16):
    return jax.ShapeDtypeStruct(shape, dtype)


def join_kernel(first, middle, last, out):
    out[:, :640] = first[...]
    for n in range(3):
        out[:, 640 * n + 640 : 640 * n + 1280] = middle[n]
    out[:, 2560:] = last[...]


def bundle_kernel(cuts, *refs):
    x, z, yh, _, c = coordinates()
    position = jnp.where(c == 0, z, x)
    outs = refs[-len(cuts) :]
    for lane in range(2):
        own, ahead, behind, low, high = refs[5 * lane : 5 * lane + 5]
        row = (yh + lane) % 2
        for out, (lower, width) in zip(outs, cuts):
            cols = slice(lower, lower + width)
            out[position, row] = own[:, cols]
            out[(position + 1) % 4, row] = ahead[:, cols]
            out[(position + 3) % 4, row] = behind[:, cols]
            split = min(max(HALF - lower, 0), width)
            if split > 0:
                out[(position + 2) % 4, row, :, :split] = low[:, lower : lower + split]
            if split < width:
                start = lower + split - HALF
                out[(position + 2) % 4, row, :, split:] = high[:, start : start + width - split]


def bundles(pieces, cuts, block, name, after):
    specs = [pl.BlockSpec((80, min(block, piece.shape[1])), lambda i: (0, 0)) for piece in pieces]
    return call(
        functools.partial(bundle_kernel, cuts),
        name,
        [shape_of((4, 2, 80, width)) for _, width in cuts],
        grid=(1,),
        in_specs=specs + [ANYWHERE] * len(after),
        out_specs=[pl.BlockSpec((4, 2, 80, width), lambda i: (0, 0, 0, 0)) for _, width in cuts],
    )(*pieces, *after)


def ring_columns(block):
    ahead = send(block, ring_route(0, -1))
    behind = send(block, ring_route(0, 1))
    low = send(behind[:, :HALF], ring_route(0, 1))
    high = send(ahead[:, HALF:], ring_route(0, -1))
    return [block, ahead, behind, low, high]


def ring_direct(block):
    across = send(block, ring_route(1, 2))
    ahead = send(block, ring_route(1, -1))
    behind = send(block, ring_route(1, 1))
    return [block, ahead, across, behind]


DIRECT_SLOTS = [(0, 0, 4), (1, 0, 4), (2, 0, 4), (3, 0, 4)]
SLOTS = [(0, 0, 4), (1, 0, 4), (3, 0, 4), (2, 0, 2), (2, 2, 2)]


def halves_kernel(behind, ahead, last, out_low, out_high, out_last):
    out_low[...] = behind[...]
    out_high[...] = ahead[...]
    out_last[...] = last[...]


def ring_forward(block, last):
    ahead = send(block, ring_route(1, -1))
    behind = send(block, ring_route(1, 1))

    def part(shape, index):
        return pl.BlockSpec(shape, index)

    one, two = (1, 1, 80, 1920), (1, 2, 80, 640)
    low, high, last = call(
        halves_kernel,
        "halves",
        [shape_of((2, 2, 80, 1920))] * 2 + [shape_of(last.shape)],
        grid=(4,),
        in_specs=[
            part(one, lambda i: (i // 2, i % 2, 0, 0)),
            part(one, lambda i: (2 + i // 2, i % 2, 0, 0)),
            part(two, lambda i: (i, 0, 0, 0)),
        ],
        out_specs=[
            part(one, lambda i: (i // 2, i % 2, 0, 0)),
            part(one, lambda i: (i // 2, i % 2, 0, 0)),
            part(two, lambda i: (i, 0, 0, 0)),
        ],
    )(behind, ahead, last)
    halves = [low, high]
    low = send(low, ring_route(1, 1))
    high = send(high, ring_route(1, -1))
    return [block, ahead, behind, low, high], last, halves


def place_start(pieces, slots, lower_col, weight, sems):
    x, z, _, _, c = coordinates()
    width = weight.shape[-1]

    def start(where):
        for n, (piece, (k, lower, count)) in enumerate(zip(pieces, slots)):
            source = piece
            if piece.shape[-1] != width:
                source = piece.at[:, :, :, pl.ds(lower_col, width)]
            target = weight.at[where(k, pl.ds(lower, count))]
            pltpu.make_async_copy(source, target, sems.at[n]).start()

    @pl.when(c == 0)
    def _():
        start(lambda k, rows: ((x + k) % 4, rows))

    @pl.when(c == 1)
    def _():
        start(lambda k, rows: (rows, (z + k) % 4))


def place_wait(slots, weight, sems):
    for n, (_, lower, count) in enumerate(slots):
        target = weight.at[0, pl.ds(lower, count)]
        pltpu.make_async_copy(target, target, sems.at[n]).wait()


def softmax_values(scores, values):
    top = jnp.max(scores, axis=-1, keepdims=True)
    lifted = jnp.exp2((scores - top) * EXP2_SCALE)
    total = jnp.sum(lifted, axis=-1, keepdims=True)
    context = jnp.dot(lifted.astype(BF16), values, preferred_element_type=F32)
    return context / total


def scores_of(query, key):
    return lax.dot_general(query, key, (((1,), (1,)), ((), ())), preferred_element_type=F32)


def aligned_kernel(tile_clip, clip_frames, qkv, hidden, out_far, out_near):
    frames_own = clip_frames[tile_clip[lax.axis_index("patch")]]
    lane = lax.broadcasted_iota(jnp.int32, (1, 384), 1) // 192
    row = lax.broadcasted_iota(jnp.int32, (384, 1), 0) // 192

    def put(place, frame):
        out_near[place] = frame[:, :8].reshape(96, HD).astype(BF16)
        out_far[place] = frame[:, 8:].reshape(96, HD).astype(BF16)

    for window in range(2):
        rows = slice(window * 384, window * 384 + 384)
        scores = scores_of(qkv[0, rows], qkv[1, rows])
        scores = jnp.where(2 * window + lane < frames_own, scores, MASKED_SCORE)
        context = softmax_values(scores, qkv[2, rows])
        context = jnp.where(2 * window + row < frames_own, context, 0.0)
        context = context.reshape(2, 12, 16, HD)
        for half in range(2):
            frame = 2 * window + half
            put((frame + 3) % 4, context[half])
            put(4 + (frame + 3) % 4, hidden[frame].astype(F32))


def aligned_attention(tile_clip, clip_frames, qkv, hidden):
    spec = pl.BlockSpec((8, 96, HD), lambda j: (0, 0, j))
    return call(
        aligned_kernel,
        "aligned_attention",
        [shape_of((8, 96, 640))] * 2,
        grid=(5,),
        in_specs=[
            SMALL,
            SMALL,
            pl.BlockSpec((3, 768, HD), lambda j: (0, 0, j)),
            pl.BlockSpec((4, 12, 16, HD), lambda j: (0, 0, 0, j)),
        ],
        out_specs=[spec, spec],
    )(tile_clip, clip_frames, qkv, hidden)


def shifted_kernel(
    tile_clip, clip_frames, own_far, own_near, other_far, other_near, gain, *refs
):
    pieces, (out, normed, qkv, low, high, sems) = refs[:5], refs[-6:]
    c = coordinates()[4]
    place_start(pieces, SLOTS, 0, low, sems.at[0])
    place_start(pieces, SLOTS, 1024, high, sems.at[1])
    patch = lax.axis_index("patch")
    clip_own, clip_next = tile_clip[patch], tile_clip[(patch + 1) % NPATCH]
    frames_own, frames_next = clip_frames[clip_own], clip_frames[clip_next]

    for half, (own, other) in enumerate(((own_far, other_far), (own_near, other_near))):
        rows = slice(384 * half, 384 * half + 384)
        mine, theirs = own[...].astype(F32), other[...].astype(F32)
        squares = jnp.sum(mine * mine, axis=-1, keepdims=True) + jnp.sum(
            theirs * theirs, axis=-1, keepdims=True
        )
        scale = lax.rsqrt(squares * (1.0 / 2560) + EPSILON)
        for a in range(2):
            for source, core in ((mine, c), (theirs, 1 - c)):
                lower = pl.multiple_of((2 * a + core) * 640, 128)
                part = source[:, a * 640 : (a + 1) * 640] * scale * gain[:, pl.ds(lower, 640)]
                normed[rows, pl.ds(lower, 640)] = part.astype(BF16)

    def project(weight, width):
        return jnp.dot(
            normed[...], weight[...].reshape(2560, width), preferred_element_type=F32
        ).astype(BF16)

    place_wait(SLOTS, low, sems.at[0])
    qkv[:, :1024] = project(low, 1024)
    place_wait(SLOTS, high, sems.at[1])
    qkv[:, 1024:] = project(high, 896)

    lane = lax.broadcasted_iota(jnp.int32, (1, 384), 1)
    row = lax.broadcasted_iota(jnp.int32, (384, 1), 0)
    alike = ((lane < 192) == (row < 192)) | (clip_own == clip_next)
    for window in range(2):
        first, second = ((1, 2), (3, 0))[window]
        far = slice(192 * window, 192 * window + 192)
        near = slice(384 + 192 * window, 384 + 192 * window + 192)

        def live(position):
            frame = jnp.where(position // 96 % 2 == 0, first, second)
            return frame < jnp.where(position < 192, frames_own, frames_next)

        allowed = alike & live(lane)
        live_rows = live(row)
        for head in range(5):
            query, key, value = [
                jnp.concatenate([qkv[far, cols], qkv[near, cols]], axis=0)
                for cols in [
                    slice(640 * n + head * HD, 640 * n + head * HD + HD) for n in range(3)
                ]
            ]
            scores = jnp.where(allowed, scores_of(query, key), MASKED_SCORE)
            context = softmax_values(scores, value)
            context = jnp.where(live_rows, context, 0.0).astype(BF16)
            cols = slice(head * HD, head * HD + HD)
            out[far, cols] = context[:192]
            out[near, cols] = context[192:]


def shifted_attention(tile_clip, clip_frames, blocks, gain, pieces):
    return call(
        shifted_kernel,
        "shifted_attention",
        shape_of((768, 640)),
        in_specs=[SMALL, SMALL] + [INSIDE] * 5 + [ANYWHERE] * 5,
        scratch_shapes=[
            pltpu.VMEM((768, 2560), BF16),
            pltpu.VMEM((768, 1920), BF16),
            pltpu.VMEM((4, 4, 2, 80, 1024), BF16),
            pltpu.VMEM((4, 4, 2, 80, 896), BF16),
            pltpu.SemaphoreType.DMA((2, 5)),
        ],
    )(tile_clip, clip_frames, *blocks, gain, *pieces)


def project_rows(rows, pieces, extra, out_send, out_keep, weight, sems):
    _, _, _, yl, c = coordinates()
    i = pl.program_id(0)

    @pl.when(i == 0)
    def _():
        place_start(pieces, DIRECT_SLOTS, 0, weight, sems)
        place_wait(DIRECT_SLOTS, weight, sems)

    part = lax.dot_general(
        rows[...].reshape(384, 640),
        weight[2 * (i % 2) + jnp.where(i < 2, 1 - c, c)].reshape(640, 640),
        (((1,), (1,)), ((), ())),
        preferred_element_type=F32,
    )

    @pl.when(i < 2)
    def _():
        out_send[...] = part.astype(BF16)

    @pl.when(i - 2 == yl)
    def _():
        out_keep[...] = (part + extra().astype(F32)).astype(BF16)

    @pl.when((i >= 2) & (i - 2 != yl))
    def _():
        out_keep[...] = part.astype(BF16)


def project_first_kernel(rows, hidden, *refs):
    project_rows(rows, refs[:4], lambda: hidden[...].reshape(384, 640), *refs[-4:])


def project_second_kernel(rows, full, *refs):
    def extra():
        return full[:, pl.ds(pl.multiple_of(coordinates()[3] * 640, 128), 640)]

    project_rows(rows, refs[:4], extra, *refs[-4:])


def project(kernel, name, operands, specs, pieces, after):
    return call(
        kernel,
        name,
        [shape_of((384, 1280))] * 2,
        grid=(4,),
        in_specs=specs + [ANYWHERE] * (len(pieces) + len(after)),
        out_specs=[
            pl.BlockSpec((384, 640), lambda i: (0, jnp.minimum(i, 1))),
            pl.BlockSpec((384, 640), lambda i: (0, jnp.maximum(i - 2, 0))),
        ],
        scratch_shapes=[pltpu.VMEM((4, 4, 2, 80, 640), BF16), pltpu.SemaphoreType.DMA((4,))],
    )(*operands, *pieces, *after)


def project_first(side, pieces, after):
    specs = [pl.BlockSpec((4, 96, 640), lambda i, n=n: (n, 0, 0)) for n in range(2)]
    return project(project_first_kernel, "project_first", (side, side), specs, pieces, after)


def project_second(side, rows, full, pieces, after):
    specs = [
        pl.BlockSpec((384, 640), lambda i: (side, 0)),
        pl.BlockSpec((384, 1280), lambda i: (0, 0)),
    ]
    return project(project_second_kernel, "project_second", (rows, full), specs, pieces, after)


def sum_kernel(count, *refs):
    refs[-1][...] = sum(ref[...].astype(F32) for ref in refs[:count]).astype(BF16)


def sums(name, terms, after):
    spec = pl.BlockSpec((128, 1280), lambda i: (i, 0))
    return call(
        functools.partial(sum_kernel, len(terms)),
        name,
        shape_of((384, 1280)),
        grid=(3,),
        in_specs=[spec] * len(terms) + [ANYWHERE] * len(after),
        out_specs=spec,
    )(*terms, *after)


def blocks_of(yl):
    return [pl.ds(pl.multiple_of(block * 640, 128), 640) for block in (yl, 1 - yl)]


def near_rows_kernel(keep, recv, *outs):
    mine, _ = blocks_of(coordinates()[3])
    for n, out in enumerate(outs):
        rows = slice(192 * n, 192 * n + 192)
        out[...] = (keep[rows, mine].astype(F32) + recv[rows, mine].astype(F32)).astype(BF16)


def near_sum_kernel(n, keep, recv, pair, out):
    _, other = blocks_of(coordinates()[3])
    rows = slice(192 * n, 192 * n + 192)
    total = keep[rows, other].astype(F32) + recv[rows, other].astype(F32)
    out[...] = (total + pair[...].astype(F32)).astype(BF16)


def far_rows_kernel(keep, recv, own, to_pair):
    mine, other = blocks_of(coordinates()[3])
    own[...] = keep[:, mine].astype(F32) + recv[:, mine].astype(F32)
    to_pair[...] = (keep[:, other].astype(F32) + recv[:, other].astype(F32)).astype(BF16)


def final_kernel(own, pair, near_0, near_1, out):
    i = pl.program_id(0)
    far = (own[...] + pair[...].astype(F32)).reshape(12, 8, 640)
    near = jnp.where(i < 2, near_0[...].astype(F32), near_1[...].astype(F32))
    out[0] = jnp.concatenate([near.reshape(12, 8, 640), far], axis=1)


def final_rows(*operands):
    rows = pl.BlockSpec((96, 640), lambda i: (i, 0))
    return call(
        final_kernel,
        "final_rows",
        shape_of((4, 12, 16, 640), F32),
        grid=(4,),
        in_specs=[
            rows,
            rows,
            pl.BlockSpec((96, 640), lambda i: (jnp.minimum(i, 1), 0)),
            pl.BlockSpec((96, 640), lambda i: (jnp.maximum(i - 2, 0), 0)),
        ],
        out_specs=pl.BlockSpec((1, 12, 16, 640), lambda i: ((i + 1) % 4, 0, 0, 0)),
    )(*operands)


def shards(hidden, qkv_first, wo_first, norm_gain, wqkv_second, wo_second, tile_clip, clip_frames):
    blocks = call(join_kernel, "join", shape_of((80, 3200)))(
        wo_first, jnp.transpose(wqkv_second, (1, 0, 2)), wo_second
    )
    partner = send(blocks, route(dyh=1))
    far, near = aligned_attention(tile_clip, clip_frames, qkv_first.reshape(3, 768, 640), hidden)
    near = send(near, tile_route(-1, 0))
    rings = ring_columns(blocks) + ring_columns(partner)
    (bundle,) = bundles(rings, [FIRST], 640, "bundle_first", [])
    first = ring_direct(bundle)
    middle, last = bundles(rings, [MIDDLE, LAST], 3200, "bundle_rest", [])
    middle, last, halves = ring_forward(middle, last)
    last = ring_direct(last)
    gain = norm_gain.reshape(1, 2560)

    fulls, chip, pair = [], [], []
    for side in (far, near):
        last_side = side is near
        to_core, keep = project_first(side, first, [chip] if last_side else [])
        recv = send(to_core, route(dc=1))
        chip = sums("chip_sum", [keep, recv], [] if last_side else [near])
        pair = send(chip, route(dyl=1))
        fulls.append(sums("block_sum", [chip, pair], [] if last_side else halves))
    blocks = fulls + [send(full, route(dc=1)) for full in fulls]
    rows = shifted_attention(tile_clip, clip_frames, blocks, gain, middle)

    low_rows = shape_of((384, 640))
    to_core, near_keep = project_second(1, rows, fulls[1], last, [])
    near_recv = send(to_core, route(dc=1))
    half_rows = shape_of((192, 640))
    pairs = call(near_rows_kernel, "near_rows", [half_rows] * 2)(near_keep, near_recv)
    to_core, keep = project_second(0, rows, fulls[0], last, [])
    own, pair_far = call(far_rows_kernel, "far_rows", [shape_of((384, 640), F32), low_rows])(
        keep, send(to_core, route(dc=1))
    )
    nears = []
    for n, pair in enumerate(pairs):
        total = call(functools.partial(near_sum_kernel, n), "near_sum", half_rows)(
            near_keep, near_recv, send(pair, route(dyl=1))
        )
        nears.append(send(total, tile_route(1, 1)))
    return final_rows(own, send(pair_far, route(dyl=1)), *nears)


def solution(mesh):
    in_specs = (
        P(None, None, "patch", "head"),
        P(None, None, None, "patch", "head"),
        P("patch", "head"),
        P(),
        P("patch", None, "head"),
        P("patch", "head"),
        P(),
        P(),
    )
    out_specs = P(None, None, "patch", "head")
    return jax.shard_map(shards, mesh=mesh, in_specs=in_specs, out_specs=out_specs, check_vma=False)
```

```python
import functools
import math

import jax
import jax.numpy as jnp
from jax import lax
from jax.experimental import pallas as pl
from jax.experimental.pallas import tpu as pltpu
from jax.sharding import PartitionSpec as P

HD = 128
EPSILON = 1e-06
MASKED_SCORE = -1e30
EXP2_SCALE = math.log2(math.e) / math.sqrt(HD)
BF16 = jnp.bfloat16
F32 = jnp.float32
AXES = ("patch", "head")
NX, NZ, NPATCH, NDEV = 4, 4, 32, 128
FIRST, MIDDLE, LAST = (0, 640), (640, 1920), (2560, 640)
HALF = 1664
VMEM_MIB = {
    "join": 4,
    "aligned_attention": 12,
    "bundle_first": 6,
    "hidden_halves": 4,
    "bundle_rest": 18,
    "halves": 6,
    "project_first": 16,
    "shifted_attention": 40,
    "project_second": 16,
    "chip_sum": 5,
    "block_sum": 5,
    "near_rows": 6,
    "near_sum": 6,
    "far_rows": 6,
    "final_rows": 6,
}
MODEL_US = {
    "join": 2,
    "aligned_attention": 6,
    "bundle_first": 2,
    "hidden_halves": 2,
    "bundle_rest": 3,
    "halves": 1,
    "project_first": 30,
    "shifted_attention": 10,
    "project_second": 6,
    "chip_sum": 2,
    "block_sum": 2,
    "near_rows": 1,
    "near_sum": 1,
    "far_rows": 1,
    "final_rows": 3,
}
ANYWHERE = pl.BlockSpec(memory_space=pl.ANY)
INSIDE = pl.BlockSpec(memory_space=pltpu.VMEM)
SMALL = pl.BlockSpec(memory_space=pltpu.SMEM)


def coordinates():
    patch, head = lax.axis_index("patch"), lax.axis_index("head")
    return patch // 8, patch // 2 % 4, patch % 2, head // 2, head % 2


def device_of(x, z, yh, yl, c):
    return ((((x % NX) * NZ + z % NZ) * 2 + yh % 2) * 2 + yl % 2) * 2 + c % 2


def route(dyh=0, dyl=0, dc=0):
    pairs = []
    for i in range(NDEV):
        c, yl, yh, z, x = i % 2, i // 2 % 2, i // 4 % 2, i // 8 % 4, i // 32
        pairs.append((i, device_of(x, z, yh + dyh, yl + dyl, c + dc)))
    return pairs


def ring_route(stage, step):
    pairs = []
    for i in range(NDEV):
        c, yl, yh, z, x = i % 2, i // 2 % 2, i // 4 % 2, i // 8 % 4, i // 32
        dx, dz = (step, 0) if (c + stage) % 2 else (0, step)
        pairs.append((i, device_of(x + dx, z + dz, yh, yl, c)))
    return pairs


def tile_route(step, flip):
    return [(i, ((i + 4 * step) % NDEV) ^ (2 * flip)) for i in range(NDEV)]


def send(block, pairs):
    return lax.ppermute(block, AXES, pairs)


def call(kernel, name, out_shape, **more):
    return pl.pallas_call(
        kernel,
        out_shape=out_shape,
        compiler_params=pltpu.CompilerParams(vmem_limit_bytes=VMEM_MIB[name] << 20),
        cost_estimate=pl.CostEstimate(
            flops=1150000000 * MODEL_US[name], bytes_accessed=1024, transcendentals=0
        ),
        name=name,
        **more,
    )


def shape_of(shape, dtype=BF16):
    return jax.ShapeDtypeStruct(shape, dtype)


def join_kernel(first, middle, last, out):
    out[:, :640] = first[...]
    for n in range(3):
        out[:, 640 * n + 640 : 640 * n + 1280] = middle[n]
    out[:, 2560:] = last[...]


def bundle_kernel(cuts, *refs):
    x, z, yh, _, c = coordinates()
    position = jnp.where(c == 0, z, x)
    outs = refs[-len(cuts) :]
    for lane in range(2):
        own, ahead, behind, low, high = refs[5 * lane : 5 * lane + 5]
        row = (yh + lane) % 2
        for out, (lower, width) in zip(outs, cuts):
            cols = slice(lower, lower + width)
            out[position, row] = own[:, cols]
            out[(position + 1) % 4, row] = ahead[:, cols]
            out[(position + 3) % 4, row] = behind[:, cols]
            split = min(max(HALF - lower, 0), width)
            if split > 0:
                out[(position + 2) % 4, row, :, :split] = low[:, lower : lower + split]
            if split < width:
                start = lower + split - HALF
                out[(position + 2) % 4, row, :, split:] = high[:, start : start + width - split]


def bundles(pieces, cuts, block, name, after):
    specs = [pl.BlockSpec((80, min(block, piece.shape[1])), lambda i: (0, 0)) for piece in pieces]
    return call(
        functools.partial(bundle_kernel, cuts),
        name,
        [shape_of((4, 2, 80, width)) for _, width in cuts],
        grid=(1,),
        in_specs=specs + [ANYWHERE] * len(after),
        out_specs=[pl.BlockSpec((4, 2, 80, width), lambda i: (0, 0, 0, 0)) for _, width in cuts],
    )(*pieces, *after)


def ring_columns(block):
    ahead = send(block, ring_route(0, -1))
    behind = send(block, ring_route(0, 1))
    low = send(behind[:, :HALF], ring_route(0, 1))
    high = send(ahead[:, HALF:], ring_route(0, -1))
    return [block, ahead, behind, low, high]


def ring_direct(block):
    across = send(block, ring_route(1, 2))
    ahead = send(block, ring_route(1, -1))
    behind = send(block, ring_route(1, 1))
    return [block, ahead, across, behind]


DIRECT_SLOTS = [(0, 0, 4), (1, 0, 4), (2, 0, 4), (3, 0, 4)]
SLOTS = [(0, 0, 4), (1, 0, 4), (3, 0, 4), (2, 0, 2), (2, 2, 2)]


def halves_kernel(behind, ahead, last, out_low, out_high, out_last):
    out_low[...] = behind[...]
    out_high[...] = ahead[...]
    out_last[...] = last[...]


def ring_forward(block, last):
    ahead = send(block, ring_route(1, -1))
    behind = send(block, ring_route(1, 1))

    def part(shape, index):
        return pl.BlockSpec(shape, index)

    one, two = (1, 1, 80, 1920), (1, 2, 80, 640)
    low, high, last = call(
        halves_kernel,
        "halves",
        [shape_of((2, 2, 80, 1920))] * 2 + [shape_of(last.shape)],
        grid=(4,),
        in_specs=[
            part(one, lambda i: (i // 2, i % 2, 0, 0)),
            part(one, lambda i: (2 + i // 2, i % 2, 0, 0)),
            part(two, lambda i: (i, 0, 0, 0)),
        ],
        out_specs=[
            part(one, lambda i: (i // 2, i % 2, 0, 0)),
            part(one, lambda i: (i // 2, i % 2, 0, 0)),
            part(two, lambda i: (i, 0, 0, 0)),
        ],
    )(behind, ahead, last)
    halves = [low, high]
    low = send(low, ring_route(1, 1))
    high = send(high, ring_route(1, -1))
    return [block, ahead, behind, low, high], last, halves


def place_start(pieces, slots, lower_col, weight, sems):
    x, z, _, _, c = coordinates()
    width = weight.shape[-1]

    def start(where):
        for n, (piece, (k, lower, count)) in enumerate(zip(pieces, slots)):
            source = piece
            if piece.shape[-1] != width:
                source = piece.at[:, :, :, pl.ds(lower_col, width)]
            target = weight.at[where(k, pl.ds(lower, count))]
            pltpu.make_async_copy(source, target, sems.at[n]).start()

    @pl.when(c == 0)
    def _():
        start(lambda k, rows: ((x + k) % 4, rows))

    @pl.when(c == 1)
    def _():
        start(lambda k, rows: (rows, (z + k) % 4))


def place_wait(slots, weight, sems):
    for n, (_, lower, count) in enumerate(slots):
        target = weight.at[0, pl.ds(lower, count)]
        pltpu.make_async_copy(target, target, sems.at[n]).wait()


def softmax_values(scores, values):
    top = jnp.max(scores, axis=-1, keepdims=True)
    lifted = jnp.exp2((scores - top) * EXP2_SCALE)
    with_ones = jnp.concatenate([values, jnp.ones_like(values)], axis=1)
    both = jnp.dot(lifted.astype(BF16), with_ones, preferred_element_type=F32)
    return both[:, :HD] / both[:, HD:]


def scores_of(query, key):
    return lax.dot_general(query, key, (((1,), (1,)), ((), ())), preferred_element_type=F32)


def aligned_kernel(tile_clip, clip_frames, qkv, hidden, out_far, out_near):
    frames_own = clip_frames[tile_clip[lax.axis_index("patch")]]
    lane = lax.broadcasted_iota(jnp.int32, (1, 384), 1) // 192
    row = lax.broadcasted_iota(jnp.int32, (384, 1), 0) // 192

    def put(place, frame):
        out_near[place] = frame[:, :8].reshape(96, HD).astype(BF16)
        out_far[place] = frame[:, 8:].reshape(96, HD).astype(BF16)

    for window in range(2):
        rows = slice(window * 384, window * 384 + 384)
        scores = scores_of(qkv[0, rows], qkv[1, rows])
        scores = jnp.where(2 * window + lane < frames_own, scores, MASKED_SCORE)
        context = softmax_values(scores, qkv[2, rows])
        context = jnp.where(2 * window + row < frames_own, context, 0.0)
        context = context.reshape(2, 12, 16, HD)
        for half in range(2):
            frame = 2 * window + half
            put((frame + 3) % 4, context[half])
            put(4 + (frame + 3) % 4, hidden[frame].astype(F32))


def aligned_attention(tile_clip, clip_frames, qkv, hidden):
    spec = pl.BlockSpec((8, 96, HD), lambda j: (0, 0, j))
    return call(
        aligned_kernel,
        "aligned_attention",
        [shape_of((8, 96, 640))] * 2,
        grid=(5,),
        in_specs=[
            SMALL,
            SMALL,
            pl.BlockSpec((3, 768, HD), lambda j: (0, 0, j)),
            pl.BlockSpec((4, 12, 16, HD), lambda j: (0, 0, 0, j)),
        ],
        out_specs=[spec, spec],
    )(tile_clip, clip_frames, qkv, hidden)


def shifted_kernel(
    tile_clip, clip_frames, own_far, own_near, other_far, other_near, gain, *refs
):
    pieces, (out, normed, qkv, low, high, sems) = refs[:5], refs[-6:]
    c = coordinates()[4]
    place_start(pieces, SLOTS, 0, low, sems.at[0])
    place_start(pieces, SLOTS, 1024, high, sems.at[1])
    patch = lax.axis_index("patch")
    clip_own, clip_next = tile_clip[patch], tile_clip[(patch + 1) % NPATCH]
    frames_own, frames_next = clip_frames[clip_own], clip_frames[clip_next]

    for half, (own, other) in enumerate(((own_far, other_far), (own_near, other_near))):
        rows = slice(384 * half, 384 * half + 384)
        mine, theirs = own[...].astype(F32), other[...].astype(F32)
        squares = jnp.sum(mine * mine, axis=-1, keepdims=True) + jnp.sum(
            theirs * theirs, axis=-1, keepdims=True
        )
        scale = lax.rsqrt(squares * (1.0 / 2560) + EPSILON)
        for a in range(2):
            for source, core in ((mine, c), (theirs, 1 - c)):
                lower = pl.multiple_of((2 * a + core) * 640, 128)
                part = source[:, a * 640 : (a + 1) * 640] * scale * gain[:, pl.ds(lower, 640)]
                normed[rows, pl.ds(lower, 640)] = part.astype(BF16)

    def project(weight, width):
        return jnp.dot(
            normed[...], weight[...].reshape(2560, width), preferred_element_type=F32
        ).astype(BF16)

    place_wait(SLOTS, low, sems.at[0])
    qkv[:, :1024] = project(low, 1024)
    place_wait(SLOTS, high, sems.at[1])
    qkv[:, 1024:] = project(high, 896)

    lane = lax.broadcasted_iota(jnp.int32, (1, 384), 1)
    row = lax.broadcasted_iota(jnp.int32, (384, 1), 0)
    alike = ((lane < 192) == (row < 192)) | (clip_own == clip_next)
    for window in range(2):
        first, second = ((1, 2), (3, 0))[window]
        far = slice(192 * window, 192 * window + 192)
        near = slice(384 + 192 * window, 384 + 192 * window + 192)

        def live(position):
            frame = jnp.where(position // 96 % 2 == 0, first, second)
            return frame < jnp.where(position < 192, frames_own, frames_next)

        allowed = alike & live(lane)
        live_rows = live(row)
        for head in range(5):
            query, key, value = [
                jnp.concatenate([qkv[far, cols], qkv[near, cols]], axis=0)
                for cols in [
                    slice(640 * n + head * HD, 640 * n + head * HD + HD) for n in range(3)
                ]
            ]
            scores = jnp.where(allowed, scores_of(query, key), MASKED_SCORE)
            context = softmax_values(scores, value)
            context = jnp.where(live_rows, context, 0.0).astype(BF16)
            cols = slice(head * HD, head * HD + HD)
            out[far, cols] = context[:192]
            out[near, cols] = context[192:]


def shifted_attention(tile_clip, clip_frames, blocks, gain, pieces):
    return call(
        shifted_kernel,
        "shifted_attention",
        shape_of((768, 640)),
        in_specs=[SMALL, SMALL] + [INSIDE] * 5 + [ANYWHERE] * 5,
        scratch_shapes=[
            pltpu.VMEM((768, 2560), BF16),
            pltpu.VMEM((768, 1920), BF16),
            pltpu.VMEM((4, 4, 2, 80, 1024), BF16),
            pltpu.VMEM((4, 4, 2, 80, 896), BF16),
            pltpu.SemaphoreType.DMA((2, 5)),
        ],
    )(tile_clip, clip_frames, *blocks, gain, *pieces)


def project_rows(rows, pieces, extra, out_send, out_keep, weight, sems):
    _, _, _, yl, c = coordinates()
    i = pl.program_id(0)

    @pl.when(i == 0)
    def _():
        place_start(pieces, DIRECT_SLOTS, 0, weight, sems)
        place_wait(DIRECT_SLOTS, weight, sems)

    part = lax.dot_general(
        rows[...].reshape(384, 640),
        weight[2 * (i % 2) + jnp.where(i < 2, 1 - c, c)].reshape(640, 640),
        (((1,), (1,)), ((), ())),
        preferred_element_type=F32,
    )

    @pl.when(i < 2)
    def _():
        out_send[...] = part.astype(BF16)

    @pl.when(i - 2 == yl)
    def _():
        out_keep[...] = (part + extra().astype(F32)).astype(BF16)

    @pl.when((i >= 2) & (i - 2 != yl))
    def _():
        out_keep[...] = part.astype(BF16)


def project_first_kernel(rows, hidden, *refs):
    project_rows(rows, refs[:4], lambda: hidden[...].reshape(384, 640), *refs[-4:])


def project_second_kernel(rows, full, *refs):
    def extra():
        return full[:, pl.ds(pl.multiple_of(coordinates()[3] * 640, 128), 640)]

    project_rows(rows, refs[:4], extra, *refs[-4:])


def project(kernel, name, operands, specs, pieces, after):
    return call(
        kernel,
        name,
        [shape_of((384, 1280))] * 2,
        grid=(4,),
        in_specs=specs + [ANYWHERE] * (len(pieces) + len(after)),
        out_specs=[
            pl.BlockSpec((384, 640), lambda i: (0, jnp.minimum(i, 1))),
            pl.BlockSpec((384, 640), lambda i: (0, jnp.maximum(i - 2, 0))),
        ],
        scratch_shapes=[pltpu.VMEM((4, 4, 2, 80, 640), BF16), pltpu.SemaphoreType.DMA((4,))],
    )(*operands, *pieces, *after)


def project_first(side, pieces, after):
    specs = [pl.BlockSpec((4, 96, 640), lambda i, n=n: (n, 0, 0)) for n in range(2)]
    return project(project_first_kernel, "project_first", (side, side), specs, pieces, after)


def project_second(side, rows, full, pieces, after):
    specs = [
        pl.BlockSpec((384, 640), lambda i: (side, 0)),
        pl.BlockSpec((384, 1280), lambda i: (0, 0)),
    ]
    return project(project_second_kernel, "project_second", (rows, full), specs, pieces, after)


def sum_kernel(count, *refs):
    refs[-1][...] = sum(ref[...].astype(F32) for ref in refs[:count]).astype(BF16)


def sums(name, terms, after):
    spec = pl.BlockSpec((128, 1280), lambda i: (i, 0))
    return call(
        functools.partial(sum_kernel, len(terms)),
        name,
        shape_of((384, 1280)),
        grid=(3,),
        in_specs=[spec] * len(terms) + [ANYWHERE] * len(after),
        out_specs=spec,
    )(*terms, *after)


def blocks_of(yl):
    return [pl.ds(pl.multiple_of(block * 640, 128), 640) for block in (yl, 1 - yl)]


def near_rows_kernel(keep, recv, *outs):
    mine, _ = blocks_of(coordinates()[3])
    for n, out in enumerate(outs):
        rows = slice(192 * n, 192 * n + 192)
        out[...] = (keep[rows, mine].astype(F32) + recv[rows, mine].astype(F32)).astype(BF16)


def near_sum_kernel(n, keep, recv, pair, out):
    _, other = blocks_of(coordinates()[3])
    rows = slice(192 * n, 192 * n + 192)
    total = keep[rows, other].astype(F32) + recv[rows, other].astype(F32)
    out[...] = (total + pair[...].astype(F32)).astype(BF16)


def far_rows_kernel(keep, recv, own, to_pair):
    mine, other = blocks_of(coordinates()[3])
    own[...] = keep[:, mine].astype(F32) + recv[:, mine].astype(F32)
    to_pair[...] = (keep[:, other].astype(F32) + recv[:, other].astype(F32)).astype(BF16)


def final_kernel(own, pair, near_0, near_1, out):
    i = pl.program_id(0)
    far = (own[...] + pair[...].astype(F32)).reshape(12, 8, 640)
    near = jnp.where(i < 2, near_0[...].astype(F32), near_1[...].astype(F32))
    out[0] = jnp.concatenate([near.reshape(12, 8, 640), far], axis=1)


def final_rows(*operands):
    rows = pl.BlockSpec((96, 640), lambda i: (i, 0))
    return call(
        final_kernel,
        "final_rows",
        shape_of((4, 12, 16, 640), F32),
        grid=(4,),
        in_specs=[
            rows,
            rows,
            pl.BlockSpec((96, 640), lambda i: (jnp.minimum(i, 1), 0)),
            pl.BlockSpec((96, 640), lambda i: (jnp.maximum(i - 2, 0), 0)),
        ],
        out_specs=pl.BlockSpec((1, 12, 16, 640), lambda i: ((i + 1) % 4, 0, 0, 0)),
    )(*operands)


def shards(hidden, qkv_first, wo_first, norm_gain, wqkv_second, wo_second, tile_clip, clip_frames):
    blocks = call(join_kernel, "join", shape_of((80, 3200)))(
        wo_first, jnp.transpose(wqkv_second, (1, 0, 2)), wo_second
    )
    partner = send(blocks, route(dyh=1))
    far, near = aligned_attention(tile_clip, clip_frames, qkv_first.reshape(3, 768, 640), hidden)
    near = send(near, tile_route(-1, 0))
    rings = ring_columns(blocks) + ring_columns(partner)
    (bundle,) = bundles(rings, [FIRST], 640, "bundle_first", [])
    first = ring_direct(bundle)
    middle, last = bundles(rings, [MIDDLE, LAST], 3200, "bundle_rest", [])
    middle, last, halves = ring_forward(middle, last)
    last = ring_direct(last)
    gain = norm_gain.reshape(1, 2560)

    fulls, chip, pair = [], [], []
    for side in (far, near):
        last_side = side is near
        to_core, keep = project_first(side, first, [chip] if last_side else [])
        recv = send(to_core, route(dc=1))
        chip = sums("chip_sum", [keep, recv], [] if last_side else [near])
        pair = send(chip, route(dyl=1))
        fulls.append(sums("block_sum", [chip, pair], [] if last_side else halves))
    blocks = fulls + [send(full, route(dc=1)) for full in fulls]
    rows = shifted_attention(tile_clip, clip_frames, blocks, gain, middle)

    low_rows = shape_of((384, 640))
    to_core, near_keep = project_second(1, rows, fulls[1], last, [])
    near_recv = send(to_core, route(dc=1))
    half_rows = shape_of((192, 640))
    pairs = call(near_rows_kernel, "near_rows", [half_rows] * 2)(near_keep, near_recv)
    to_core, keep = project_second(0, rows, fulls[0], last, [])
    own, pair_far = call(far_rows_kernel, "far_rows", [shape_of((384, 640), F32), low_rows])(
        keep, send(to_core, route(dc=1))
    )
    nears = []
    for n, pair in enumerate(pairs):
        total = call(functools.partial(near_sum_kernel, n), "near_sum", half_rows)(
            near_keep, near_recv, send(pair, route(dyl=1))
        )
        nears.append(send(total, tile_route(1, 1)))
    return final_rows(own, send(pair_far, route(dyl=1)), *nears)


def solution(mesh):
    in_specs = (
        P(None, None, "patch", "head"),
        P(None, None, None, "patch", "head"),
        P("patch", "head"),
        P(),
        P("patch", None, "head"),
        P("patch", "head"),
        P(),
        P(),
    )
    out_specs = P(None, None, "patch", "head")
    return jax.shard_map(shards, mesh=mesh, in_specs=in_specs, out_specs=out_specs, check_vma=False)
```
